256 devices in a mesh: dp: 32 (over z, x), seq: 2 (over core), tensor: 4 (over y).
Axes of the slice: x: 4, y: 4, z: 8, core: 2. Of those that a mesh axis runs over, the one named last changes fastest.
Arguments:
- tokens: bfloat16 [32, 2048, 8192], P('dp', 'seq', 'tensor'), may hold values from -6 to 6
- input_map: bfloat16 [32, 2048, 512], P('dp', 'seq', 'tensor'), may hold values from -0.5 to 0.5
- output_map: bfloat16 [32, 2048, 512], P('dp', 'seq', 'tensor'), may hold values from -0.5 to 0.5
- log_decay: float32 [32, 128, 2048], P('dp', 'tensor', 'seq'), may hold values from -2 to 0, as said below
- step_size: float32 [32, 128, 2048], P('dp', 'tensor', 'seq'), may hold values from 0.05 to 0.2
- skip_gain: float32 [128], P('tensor'), may hold values from 0.5 to 1.5
- snapshots: bfloat16 [128, 128, 64, 128], P(('dp', 'seq'), 'tensor'), may hold values from -3 to 3
- first_snap: int32 [32], replicated, may hold values from 0 to 120
- prefix_kilo: int32 [32], replicated, may hold values from 1 to 8
- snap_slot: int32 [128], replicated, may hold values from 0 to 127, each once
Outputs:
- scan_out: bfloat16 [32, 2048, 8192], P('dp', ('seq', 'tensor'))
The draws below stay inside these ranges and needn't reach their ends.
Inputs may be any that keep to these rules, and one draw needn't show every extreme that they name: A request's conversation has catalogue entries first_snap to first_snap + 7. Request r reloads catalogue entry first_snap[r] + prefix_kilo[r] - 1. `snap_slot`: each slot appears once; slot k is row k of snapshots. `log_decay`: strictly negative.
All inputs are finite; a program needn't handle non-finite values.
Results may differ from the reference program's by a relative error of at most 0.005.
Values may be sent and summed in bfloat16 or wider, within the bound.
A program may use at most 192 MiB of HBM per device.

```python
import math
import jax
import jax.numpy as jnp
from jax import lax

HEADS = 128
GROUPS = 4
HEAD_DIM = 64
STATE = 128
BLOCK = 128
MAXK = 8
SUFFIX = 2048
REQUESTS = 32
SNAPS = 128


def draw_log_decay(key, part):
    key = jax.random.fold_in(key, 17)
    keys = jax.random.split(key, 6)
    fast_share = 0.5
    head_shape = (REQUESTS, HEADS, 1)
    fast_heads = (jax.random.uniform(keys[0], head_shape) < fast_share).astype(jnp.float32)
    fast_rate = jnp.exp(jax.random.uniform(keys[1], head_shape, minval=math.log(0.045), maxval=math.log(0.08)))
    slow_rate = jax.random.uniform(keys[2], head_shape, minval=0.2, maxval=0.8) / SUFFIX
    baseline_rate = fast_heads * fast_rate + (1.0 - fast_heads) * slow_rate
    jaggedness = jnp.exp(jax.random.uniform(keys[3], (REQUESTS, HEADS, SUFFIX), minval=math.log(0.5), maxval=math.log(2.0))) / 1.0821
    places = jax.random.randint(keys[4], (REQUESTS, 1, 2), 0, SUFFIX)
    loss_values = jax.random.uniform(keys[5], (REQUESTS, HEADS, 2), minval=0.2, maxval=0.5)
    position = jnp.arange(SUFFIX, dtype=jnp.int32)
    match_count = position[None, None, None, :] == places[..., None]
    spike_events = jnp.sum(jnp.where(match_count, jnp.log(1.0 - loss_values)[..., None], 0.0), axis=2)
    return -(baseline_rate * jaggedness) + spike_events


def touch_ends(array, rng, smallest, high):
    spot = [jax.random.randint(jax.random.fold_in(rng, axis), (), 0, length) for axis, length in enumerate(array.shape)]
    longest = array.shape.index(max(array.shape))
    next_to = spot[:longest] + [(spot[longest] + 1) % array.shape[longest]] + spot[longest + 1:]
    return array.at[tuple(spot)].set(smallest).at[tuple(next_to)].set(high)


def level_of(key, extent, shards, smallest, high):
    gain = 1.0
    for axis_at, parts in shards:
        heights = jax.random.uniform(jax.random.fold_in(jax.random.fold_in(key, 6), axis_at), (parts,), jnp.float32, smallest / len(shards), high / len(shards))
        gain = gain * jnp.repeat(jnp.exp(heights), extent[axis_at] // parts).reshape((-1,) + (1,) * (len(extent) - 1 - axis_at))
    return gain


def gaussian(own_key, shape, scale, limit, cuts=(), held_as=jnp.bfloat16):
    drawn = scale * jax.random.normal(own_key, shape, jnp.float32)
    if cuts:
        drawn = drawn * level_of(own_key, shape, cuts, -0.22, 0.18)
    return jnp.clip(drawn, -limit, limit).astype(held_as)


def setup_inputs(seed: int = 0) -> dict:
    key_list = jax.random.split(jax.random.key(seed), 11)
    tokens = gaussian(key_list[0], (REQUESTS, SUFFIX, HEADS * HEAD_DIM), 1.0, 6.0, ((0, 32), (1, 2), (2, 4)))
    input_map = gaussian(key_list[1], (REQUESTS, SUFFIX, GROUPS * STATE), STATE ** -0.5, 0.5, ((0, 32), (1, 2), (2, 4)))
    output_map = gaussian(key_list[2], (REQUESTS, SUFFIX, GROUPS * STATE), STATE ** -0.5, 0.5, ((0, 32), (1, 2), (2, 4)))
    log_decay = draw_log_decay(jax.random.fold_in(key_list[10], 71), 0)
    step_size = jnp.clip(jnp.exp(math.log(0.2) - 1.3862944 * jax.random.uniform(key_list[4], (REQUESTS, HEADS, SUFFIX), jnp.float32) ** level_of(key_list[4], (REQUESTS, HEADS, SUFFIX), ((0, 32), (1, 4), (2, 2)), -0.2, 0.2)), 0.05, 0.2)
    skip_gain = jnp.clip(0.5 + 1.0 * jax.random.uniform(key_list[5], (HEADS,), jnp.float32) ** level_of(key_list[5], (HEADS,), ((0, 4),), -0.2, 0.2), 0.5, 1.5)
    snapshots = gaussian(key_list[6], (SNAPS, HEADS, HEAD_DIM, STATE), 0.5, 3.0, ((0, 64), (1, 4)))
    first_snap = touch_ends(jax.random.randint(key_list[7], (REQUESTS,), 0, SNAPS - MAXK + 1), jax.random.fold_in(key_list[7], 1), 0, SNAPS - MAXK).astype(jnp.int32)
    prefix_kilo = touch_ends(jax.random.randint(key_list[8], (REQUESTS,), 1, MAXK + 1), jax.random.fold_in(key_list[8], 1), 1, MAXK).astype(jnp.int32)
    snap_slot = jax.random.permutation(key_list[9], SNAPS).astype(jnp.int32)
    return dict(tokens=tokens, input_map=input_map, output_map=output_map, log_decay=log_decay, step_size=step_size, skip_gain=skip_gain, snapshots=snapshots, first_snap=first_snap, prefix_kilo=prefix_kilo, snap_slot=snap_slot)


def block_update(tokens_blk, input_blk, output_blk, decay_blk, step_blk, skip_gain, state_before):
    length = tokens_blk.shape[0]
    head_count = decay_blk.shape[0]
    groups = input_blk.shape[1] // STATE
    within_group = head_count // groups
    highest = lax.Precision.HIGHEST
    running = jnp.cumsum(decay_blk, axis=1)
    values = tokens_blk.astype(jnp.float32).reshape(length, groups, within_group, HEAD_DIM)
    inputs = input_blk.astype(jnp.float32).reshape(length, groups, STATE)
    outputs = output_blk.astype(jnp.float32).reshape(length, groups, STATE)
    scores = jnp.einsum("qgn,kgn->gqk", outputs, inputs, precision=highest)
    later_position = lax.broadcasted_iota(jnp.int32, (length, length), 0)
    earlier = lax.broadcasted_iota(jnp.int32, (length, length), 1)
    spread = jnp.minimum(running[:, :, None] - running[:, None, :], 0.0)
    falloff = jnp.where(later_position >= earlier, jnp.exp(spread), 0.0) * step_blk[:, None, :]
    weights = (scores[:, None] * falloff.reshape(groups, within_group, length, length)).astype(jnp.bfloat16)
    inner_part = jnp.einsum("gkqs,sgkp->qgkp", weights.astype(jnp.float32), values, precision=highest)
    ending = running[:, -1:]
    factor = (jnp.exp(ending - running) * step_blk).reshape(groups, within_group, length)
    scaled = (values * jnp.transpose(factor, (2, 0, 1))[..., None]).astype(jnp.bfloat16)
    state_add = jnp.einsum("qgkp,qgn->gkpn", scaled.astype(jnp.float32), inputs, precision=highest)
    state_add = state_add.reshape(head_count, HEAD_DIM, STATE)
    carried = jnp.einsum("qgn,gkpn->qgkp", outputs, state_before.reshape(groups, within_group, HEAD_DIM, STATE), precision=highest)
    growth = jnp.transpose(jnp.exp(running).reshape(groups, within_group, length), (2, 0, 1))[..., None]
    mixed_out = inner_part + carried * growth + values * skip_gain.reshape(groups, within_group)[None, :, :, None]
    state_after = jnp.exp(ending)[:, :, None] * state_before + state_add
    return mixed_out.reshape(length, head_count * HEAD_DIM), state_after


def reference(tokens, input_map, output_map, log_decay, step_size, skip_gain, snapshots, first_snap, prefix_kilo, snap_slot):
    chosen = snap_slot[(first_snap + prefix_kilo - 1).astype(jnp.int32)]
    blocks = SUFFIX // BLOCK

    def one_request(packed):
        tok_req, in_req, out_req, decay_req, step_req, slot_index = packed
        start_state = snapshots[slot_index].astype(jnp.float32)
        pieces = (
            tok_req.reshape(blocks, BLOCK, HEADS * HEAD_DIM),
            in_req.reshape(blocks, BLOCK, GROUPS * STATE),
            out_req.reshape(blocks, BLOCK, GROUPS * STATE),
            jnp.transpose(decay_req.reshape(HEADS, blocks, BLOCK), (1, 0, 2)),
            jnp.transpose(step_req.reshape(HEADS, blocks, BLOCK), (1, 0, 2)),
        )

        def advance(state_now, block_in):
            mixed_out, state_after = block_update(*block_in, skip_gain, state_now)
            return state_after, mixed_out

        final_state, mixed_all = lax.scan(advance, start_state, pieces)
        return mixed_all.reshape(SUFFIX, HEADS * HEAD_DIM).astype(jnp.bfloat16)

    return lax.map(one_request, (tokens, input_map, output_map, log_decay, step_size, chosen))
```

```python
import functools

import jax
import jax.numpy as jnp
from jax import lax
from jax.experimental import pallas as pl
from jax.experimental.pallas import tpu as pltpu
from jax.sharding import PartitionSpec as P

HEAD_DIM = 64
STATE = 128
BLOCK = 128
CHUNK = 8 * HEAD_DIM
LOG2E = 1.4426950408889634
MESH = pl.DeviceIdType.MESH
F32 = jnp.float32
BF16 = jnp.bfloat16


def prepare(blocks, b_ref, c_ref, ld_ref, dt_ref, gain_ref, sm, bt, run_t, urow, fac, rows_e):
    heads = ld_ref.shape[0]
    width = heads * HEAD_DIM
    row = lax.broadcasted_iota(jnp.int32, (BLOCK, BLOCK), 0)
    col = lax.broadcasted_iota(jnp.int32, (BLOCK, BLOCK), 1)
    upto = (row <= col).astype(F32)
    ends = []
    for b in range(blocks):
        at = pl.ds(b * BLOCK, BLOCK)
        run = jnp.dot(
            ld_ref[:, at], upto, precision=lax.Precision.HIGHEST, preferred_element_type=F32
        )
        run = run * LOG2E
        step = dt_ref[:, at]
        end = run[:, BLOCK - 1 :]
        urow[:, at] = run - jnp.log2(step)
        fac[:, at] = jnp.exp2(end - run) * step
        padded = jnp.concatenate([run, jnp.zeros((BLOCK - heads, BLOCK), F32)], axis=0)
        turned = padded.T
        run_t[at, :] = turned
        ends.append(turned[BLOCK - 1 :, :])
        inputs = b_ref[at, :]
        scores = lax.dot_general(
            c_ref[at, :], inputs, (((1,), (1,)), ((), ())), preferred_element_type=F32
        )
        sm[at, :] = jnp.where(row >= col, scores, 0.0)
        bt[at, :] = inputs.astype(F32).T
    stacked = jnp.concatenate(ends + [gain_ref[...]], axis=0)
    pad = (-stacked.shape[0]) % 8
    if pad:
        stacked = jnp.concatenate([stacked, jnp.zeros((pad, BLOCK), F32)], axis=0)
    spot = lax.broadcasted_iota(jnp.int32, (BLOCK, width), 0)
    head = lax.broadcasted_iota(jnp.int32, (BLOCK, width), 1) // HEAD_DIM
    spread = (spot == head).astype(F32)
    wide = jnp.dot(stacked, spread, precision=lax.Precision.HIGHEST, preferred_element_type=F32)
    reach = jnp.zeros((1, width), F32)
    for b in range(blocks):
        end = wide[b : b + 1, :]
        rows_e[b] = jnp.broadcast_to(jnp.exp2(end), (8, width))
        rows_e[blocks + 1 + b] = jnp.broadcast_to(jnp.exp2(reach), (8, width))
        reach = reach + end
    rows_e[blocks] = jnp.broadcast_to(wide[blocks : blocks + 1, :], (8, width))
    rows_e[2 * blocks + 1] = jnp.broadcast_to(jnp.exp2(reach), (8, width))


def local_chunk(
    blocks, k, x_ref, c_ref, sm, bt, run_t, urow, fac, rows_e, state, summary, acc, growth
):
    cols = pl.ds(pl.multiple_of(k * CHUNK, CHUNK), CHUNK)
    octet = pl.ds(pl.multiple_of(k * 8, 8), 8)
    pair_width = 2 * HEAD_DIM
    first = lax.broadcasted_iota(jnp.int32, (1, pair_width), 1) < HEAD_DIM
    keep0 = jnp.where(first, 1.0, 0.0).astype(BF16)
    keep1 = jnp.where(first, 0.0, 1.0).astype(BF16)
    state[...] = jnp.zeros_like(state)

    def one(b, _):
        at = pl.ds(pl.multiple_of(b * BLOCK, BLOCK), BLOCK)
        turned = pltpu.roll(run_t[at, :], lax.rem(BLOCK - 8 * k, BLOCK), 1)
        u = urow[octet, at]
        f = fac[octet, at]
        carried = jnp.dot(c_ref[at, :], state[...].astype(BF16), preferred_element_type=F32)
        for j in range(CHUNK // pair_width):
            mine = slice(j * pair_width, (j + 1) * pair_width)
            here = pl.ds(pl.multiple_of(k * CHUNK + j * pair_width, pair_width), pair_width)
            h0, h1 = slice(2 * j, 2 * j + 1), slice(2 * j + 1, 2 * j + 2)
            scores = sm[at, :]
            back = bt[at, :]
            run0 = jnp.broadcast_to(turned[:, h0], (BLOCK, BLOCK))
            run1 = jnp.broadcast_to(turned[:, h1], (BLOCK, BLOCK))
            w0 = (scores * jnp.exp2(jnp.minimum(run0 - u[h0], 64.0))).astype(BF16)
            w1 = (scores * jnp.exp2(jnp.minimum(run1 - u[h1], 64.0))).astype(BF16)
            b0 = (back * f[h0]).astype(BF16)
            b1 = (back * f[h1]).astype(BF16)
            x = x_ref[at, here]
            left = jnp.concatenate(
                [jnp.concatenate([w0, w1], axis=1), jnp.concatenate([b0, b1], axis=1)], axis=0
            )
            right = jnp.concatenate([x * keep0, x * keep1], axis=0)
            both = jnp.dot(left, right, preferred_element_type=F32)
            grown = jnp.exp2(jnp.where(first, run0, run1))
            acc[at, here] = (
                both[:BLOCK]
                + grown * carried[:, mine]
                + x.astype(F32) * rows_e[blocks, :, here][0:1, :]
            )
            growth[at, here] = grown * rows_e[blocks + 1 + b, :, here][0:1, :]
            state[:, mine] = rows_e[b, :, here][0:1, :] * state[:, mine] + both[BLOCK:]
        return 0

    lax.fori_loop(0, blocks, one, 0, unroll=2)
    summary[:, cols] = state[...].astype(BF16)


def kernel(
    blocks,
    ranks,
    x_ref,
    b_ref,
    c_ref,
    ld_ref,
    dt_ref,
    gain_ref,
    s0_ref,
    o_ref,
    sm,
    bt,
    run_t,
    urow,
    fac,
    rows_e,
    state,
    summary,
    acc,
    growth,
    staged,
    sum_in,
    decay_in,
    sib_send,
    sib_recv,
    y_send,
    y_recv,
    own_sem,
):
    dp, core, y = lax.axis_index("dp"), lax.axis_index("seq"), lax.axis_index("tensor")
    sibling = (dp, 1 - core, y)
    quarter = blocks * BLOCK // ranks
    width = x_ref.shape[1]
    chunks = width // CHUNK

    def peer(step):
        return (dp, core, lax.rem(y + step, ranks))

    barrier = pltpu.get_barrier_semaphore()
    pl.semaphore_signal(barrier, inc=1, device_id=sibling, device_id_type=MESH)
    for step in range(1, ranks):
        pl.semaphore_signal(barrier, inc=1, device_id=peer(step), device_id_type=MESH)
    pl.semaphore_wait(barrier, ranks)

    prepare(blocks, b_ref, c_ref, ld_ref, dt_ref, gain_ref, sm, bt, run_t, urow, fac, rows_e)
    decay_copy = pltpu.make_async_remote_copy(
        src_ref=rows_e.at[2 * blocks + 1],
        dst_ref=decay_in,
        send_sem=sib_send.at[0],
        recv_sem=sib_recv.at[0],
        device_id=sibling,
        device_id_type=MESH,
    )
    decay_copy.start()

    def run_chunk(k, _):
        local_chunk(
            blocks, k, x_ref, c_ref, sm, bt, run_t, urow, fac, rows_e, state, summary, acc, growth
        )
        return 0

    lax.fori_loop(0, chunks, run_chunk, 0)
    sum_copy = pltpu.make_async_remote_copy(
        src_ref=summary,
        dst_ref=sum_in,
        send_sem=sib_send.at[1],
        recv_sem=sib_recv.at[1],
        device_id=sibling,
        device_id_type=MESH,
    )
    sum_copy.start()
    decay_copy.wait()
    sum_copy.wait()
    later = core == 1

    def y_copy(k, step):
        cols = pl.ds(pl.multiple_of(k * CHUNK, CHUNK), CHUNK)
        there = pl.ds(pl.multiple_of(y * width + k * CHUNK, CHUNK), CHUNK)
        rows = pl.ds(pl.multiple_of(lax.rem(y + step, ranks) * quarter, quarter), quarter)
        if step == 0:
            return pltpu.make_async_copy(staged.at[rows, cols], o_ref.at[:, there], own_sem.at[k])
        return pltpu.make_async_remote_copy(
            src_ref=staged.at[rows, cols],
            dst_ref=o_ref.at[:, there],
            send_sem=y_send.at[k, step - 1],
            recv_sem=y_recv.at[k, step - 1],
            device_id=peer(step),
            device_id_type=MESH,
        )

    def finish(k, _):
        cols = pl.ds(pl.multiple_of(k * CHUNK, CHUNK), CHUNK)
        decay = jnp.where(later, decay_in[0:1, cols], 1.0)
        earlier = jnp.where(later, sum_in[:, cols].astype(F32), 0.0).astype(BF16)
        begin = s0_ref[cols, :]
        for step in (2, 1, 3, 0):
            rows = pl.ds(pl.multiple_of(lax.rem(y + step, ranks) * quarter, quarter), quarter)
            c = c_ref[rows, :]
            mixed = decay * lax.dot_general(
                c, begin, (((1,), (1,)), ((), ())), preferred_element_type=F32
            ) + jnp.dot(c, earlier, preferred_element_type=F32)
            staged[rows, cols] = (acc[rows, cols] + growth[rows, cols] * mixed).astype(BF16)
            y_copy(k, step).start()
        return 0

    lax.fori_loop(0, chunks, finish, 0)

    def drain(k, _):
        for step in range(ranks):
            y_copy(k, step).wait()
        return 0

    lax.fori_loop(0, chunks, drain, 0)


def copy_kernel(parts, in_ref, out_ref, held, in_sem, out_sem):
    rows = in_ref.shape[0] // parts

    def part(i):
        return pl.ds(i * rows, rows)

    reads = [
        pltpu.make_async_copy(in_ref.at[part(i)], held.at[part(i)], in_sem.at[i])
        for i in range(parts)
    ]
    writes = [
        pltpu.make_async_copy(held.at[part(i)], out_ref.at[part(i)], out_sem.at[i])
        for i in range(parts)
    ]
    for read in reads:
        read.start()
    for read, write in zip(reads, writes):
        read.wait()
        write.start()
    for write in writes:
        write.wait()


def start_states(snapshots, first_snap, prefix_kilo, snap_slot):
    slots_here, heads = snapshots.shape[:2]
    row_size = 2 * slots_here
    dp_count = lax.axis_size("dp")
    spread = lax.all_to_all(snapshots, "dp", split_axis=1, concat_axis=0, tiled=True)
    chosen = snap_slot[first_snap + prefix_kilo - 1]
    within = chosen % row_size
    mine = within // slots_here == lax.axis_index("seq")
    picked = spread[(chosen // row_size) * slots_here + within % slots_here]
    picked = jnp.where(mine[:, None, None, None], picked, jnp.zeros_like(picked))
    got = lax.all_to_all(picked, "dp", split_axis=0, concat_axis=1, tiled=True)
    del heads, dp_count
    return lax.psum(got, "seq")[0]


def per_device(
    tokens,
    input_map,
    output_map,
    log_decay,
    step_size,
    skip_gain,
    snapshots,
    first_snap,
    prefix_kilo,
    snap_slot,
):
    length, width = tokens.shape[1:]
    heads = log_decay.shape[1]
    blocks = length // BLOCK
    ranks = lax.axis_size("tensor")
    chunks = width // CHUNK
    begin = start_states(snapshots, first_snap, prefix_kilo, snap_slot)
    gain = jnp.pad(skip_gain, (0, BLOCK - heads)).reshape(1, BLOCK)
    out_shape = (length // ranks, width * ranks)
    vmem = pl.BlockSpec(memory_space=pltpu.VMEM)
    mixed = pl.pallas_call(
        functools.partial(kernel, blocks, ranks),
        out_shape=jax.ShapeDtypeStruct(out_shape, BF16),
        in_specs=[vmem] * 7,
        out_specs=pl.BlockSpec(memory_space=pl.ANY),
        scratch_shapes=[
            pltpu.VMEM((length, BLOCK), F32),
            pltpu.VMEM((length, BLOCK), F32),
            pltpu.VMEM((length, BLOCK), F32),
            pltpu.VMEM((heads, length), F32),
            pltpu.VMEM((heads, length), F32),
            pltpu.VMEM((2 * blocks + 2, 8, width), F32),
            pltpu.VMEM((STATE, CHUNK), F32),
            pltpu.VMEM((STATE, width), BF16),
            pltpu.VMEM((length, width), F32),
            pltpu.VMEM((length, width), F32),
            pltpu.VMEM((length, width), BF16),
            pltpu.VMEM((STATE, width), BF16),
            pltpu.VMEM((8, width), F32),
            pltpu.SemaphoreType.DMA((2,)),
            pltpu.SemaphoreType.DMA((2,)),
            pltpu.SemaphoreType.DMA((chunks, ranks - 1)),
            pltpu.SemaphoreType.DMA((chunks, ranks - 1)),
            pltpu.SemaphoreType.DMA((chunks,)),
        ],
        compiler_params=pltpu.CompilerParams(
            collective_id=0, has_side_effects=True, vmem_limit_bytes=56 * 2**20
        ),
        name="scan_and_send",
    )(
        tokens[0],
        input_map[0],
        output_map[0],
        log_decay[0],
        step_size[0],
        gain,
        begin.reshape(width, STATE),
    )
    parts = 4
    result = pl.pallas_call(
        functools.partial(copy_kernel, parts),
        out_shape=jax.ShapeDtypeStruct(out_shape, BF16),
        in_specs=[pl.BlockSpec(memory_space=pl.ANY)],
        out_specs=pl.BlockSpec(memory_space=pl.ANY),
        scratch_shapes=[
            pltpu.VMEM(out_shape, BF16),
            pltpu.SemaphoreType.DMA((parts,)),
            pltpu.SemaphoreType.DMA((parts,)),
        ],
        compiler_params=pltpu.CompilerParams(vmem_limit_bytes=16 * 2**20),
        name="place_result",
    )(mixed)
    return result[None]


def solution(mesh):
    placed = (
        P("dp", "seq", "tensor"),
        P("dp", "seq", "tensor"),
        P("dp", "seq", "tensor"),
        P("dp", "tensor", "seq"),
        P("dp", "tensor", "seq"),
        P("tensor"),
        P(("dp", "seq"), "tensor", None, None),
        P(),
        P(),
        P(),
    )
    return jax.shard_map(
        per_device,
        mesh=mesh,
        in_specs=placed,
        out_specs=P("dp", ("seq", "tensor"), None),
        check_vma=False,
    )
```

```python
import functools

import jax
import jax.numpy as jnp
from jax import lax
from jax.experimental import pallas as pl
from jax.experimental.pallas import tpu as pltpu
from jax.sharding import PartitionSpec as P

HEAD_DIM = 64
STATE = 128
BLOCK = 128
CHUNK = 8 * HEAD_DIM
LOG2E = 1.4426950408889634
ROW = 4
SPAN = 4
MESH = pl.DeviceIdType.MESH
F32 = jnp.float32
BF16 = jnp.bfloat16


def prepare(blocks, b_ref, c_ref, ld_ref, dt_ref, gain_ref, sm, bt, run_t, urow, fac, rows_e):
    heads = ld_ref.shape[0]
    width = heads * HEAD_DIM
    row = lax.broadcasted_iota(jnp.int32, (BLOCK, BLOCK), 0)
    col = lax.broadcasted_iota(jnp.int32, (BLOCK, BLOCK), 1)
    upto = (row <= col).astype(F32)
    ends = []
    for b in range(blocks):
        at = pl.ds(b * BLOCK, BLOCK)
        run = jnp.dot(
            ld_ref[:, at], upto, precision=lax.Precision.HIGHEST, preferred_element_type=F32
        )
        run = run * LOG2E
        step = dt_ref[:, at]
        end = run[:, BLOCK - 1 :]
        urow[:, at] = run - jnp.log2(step)
        fac[:, at] = jnp.exp2(end - run) * step
        padded = jnp.concatenate([run, jnp.zeros((BLOCK - heads, BLOCK), F32)], axis=0)
        turned = padded.T
        run_t[at, :] = turned
        ends.append(turned[BLOCK - 1 :, :])
        inputs = b_ref[at, :]
        scores = lax.dot_general(
            c_ref[at, :], inputs, (((1,), (1,)), ((), ())), preferred_element_type=F32
        )
        sm[at, :] = jnp.where(row >= col, scores, 0.0)
        bt[at, :] = inputs.astype(F32).T
    stacked = jnp.concatenate(ends, axis=0)
    pad = (-stacked.shape[0]) % 8
    if pad:
        stacked = jnp.concatenate([stacked, jnp.zeros((pad, BLOCK), F32)], axis=0)
    spot = lax.broadcasted_iota(jnp.int32, (BLOCK, width), 0)
    head = lax.broadcasted_iota(jnp.int32, (BLOCK, width), 1) // HEAD_DIM
    spread = (spot == head).astype(F32)
    wide = jnp.dot(stacked, spread, precision=lax.Precision.HIGHEST, preferred_element_type=F32)
    gain = jnp.dot(
        gain_ref[...], spread[:heads], precision=lax.Precision.HIGHEST, preferred_element_type=F32
    )
    reach = jnp.zeros((1, width), F32)
    for b in range(blocks):
        end = wide[b : b + 1, :]
        rows_e[b] = jnp.broadcast_to(jnp.exp2(end), (8, width))
        rows_e[blocks + 1 + b] = jnp.broadcast_to(jnp.exp2(reach), (8, width))
        reach = reach + end
    rows_e[blocks] = jnp.broadcast_to(gain, (8, width))
    rows_e[2 * blocks + 1] = jnp.broadcast_to(jnp.exp2(reach), (8, width))


def local_chunk(
    blocks, k, x_ref, c_ref, sm, bt, run_t, urow, fac, rows_e, state, summary, acc, growth
):
    cols = pl.ds(pl.multiple_of(k * CHUNK, CHUNK), CHUNK)
    octet = pl.ds(pl.multiple_of(k * 8, 8), 8)
    pair_width = 2 * HEAD_DIM
    first = lax.broadcasted_iota(jnp.int32, (1, pair_width), 1) < HEAD_DIM
    keep0 = jnp.where(first, 1.0, 0.0).astype(BF16)
    keep1 = jnp.where(first, 0.0, 1.0).astype(BF16)
    state[...] = jnp.zeros_like(state)

    def one(b, _):
        at = pl.ds(pl.multiple_of(b * BLOCK, BLOCK), BLOCK)
        turned = pltpu.roll(run_t[at, :], lax.rem(BLOCK - 8 * k, BLOCK), 1)
        u = urow[octet, at]
        f = fac[octet, at]
        carried = jnp.dot(c_ref[at, :], state[...].astype(BF16), preferred_element_type=F32)
        for j in range(CHUNK // pair_width):
            mine = slice(j * pair_width, (j + 1) * pair_width)
            here = pl.ds(pl.multiple_of(k * CHUNK + j * pair_width, pair_width), pair_width)
            h0, h1 = slice(2 * j, 2 * j + 1), slice(2 * j + 1, 2 * j + 2)
            scores = sm[at, :]
            back = bt[at, :]
            run0 = jnp.broadcast_to(turned[:, h0], (BLOCK, BLOCK))
            run1 = jnp.broadcast_to(turned[:, h1], (BLOCK, BLOCK))
            w0 = (scores * jnp.exp2(jnp.minimum(run0 - u[h0], 64.0))).astype(BF16)
            w1 = (scores * jnp.exp2(jnp.minimum(run1 - u[h1], 64.0))).astype(BF16)
            b0 = (back * f[h0]).astype(BF16)
            b1 = (back * f[h1]).astype(BF16)
            x = x_ref[at, here]
            left = jnp.concatenate(
                [jnp.concatenate([w0, w1], axis=1), jnp.concatenate([b0, b1], axis=1)], axis=0
            )
            right = jnp.concatenate([x * keep0, x * keep1], axis=0)
            both = jnp.dot(left, right, preferred_element_type=F32)
            grown = jnp.exp2(jnp.where(first, run0, run1))
            acc[at, here] = (
                both[:BLOCK]
                + grown * carried[:, mine]
                + x.astype(F32) * rows_e[blocks, :, here][0:1, :]
            )
            growth[at, here] = grown * rows_e[blocks + 1 + b, :, here][0:1, :]
            state[:, mine] = rows_e[b, :, here][0:1, :] * state[:, mine] + both[BLOCK:]
        return 0

    lax.fori_loop(0, blocks, one, 0, unroll=2)
    summary[:, cols] = state[...].astype(BF16)


def loop(start, stop, group, body):
    def step(j, _):
        for i in range(group):
            body(start + j * group + i)
        return 0

    steps = (stop - start) // group
    lax.fori_loop(0, steps, step, 0)
    for i in range(start + steps * group, stop):
        body(i)


def kernel(
    blocks,
    ranks,
    first_ref,
    prefix_ref,
    slot_ref,
    x_hbm,
    b_hbm,
    c_hbm,
    ld_hbm,
    dt_hbm,
    gain_ref,
    snap_ref,
    o_ref,
    x_ref,
    b_ref,
    c_ref,
    ld_ref,
    dt_ref,
    sm,
    bt,
    run_t,
    urow,
    fac,
    rows_e,
    state,
    summary,
    acc,
    growth,
    staged,
    sum_in,
    decay_in,
    begin,
    spread,
    held,
    picked,
    offered,
    came,
    place,
    load_sem,
    x_sem,
    spread_send,
    spread_recv,
    pick_send,
    pick_recv,
    decay_sem,
    sum_send,
    sum_recv,
    pass_send,
    pass_recv,
    y_send,
    y_recv,
    own_sem,
):
    dp, core, y = lax.axis_index("dp"), lax.axis_index("seq"), lax.axis_index("tensor")
    z, x = dp // ROW, dp % ROW
    plane = lax.axis_size("dp")
    rings = plane // ROW
    sibling = (dp, 1 - core, y)
    quarter = blocks * BLOCK // ranks
    width = x_ref.shape[1]
    chunks = width // CHUNK
    piece = CHUNK // (SPAN * ROW)

    def peer(step):
        return (dp, core, lax.rem(y + step, ranks))

    def chunk_of(k):
        return pl.ds(pl.multiple_of(k * CHUNK, CHUNK), CHUNK)

    def x_load(k):
        cols = chunk_of(k)
        return pltpu.make_async_copy(x_hbm.at[:, cols], x_ref.at[:, cols], x_sem.at[k])

    barrier = pltpu.get_barrier_semaphore()

    def greet(i):
        who = (lax.rem(dp + i // 2, plane), lax.rem(core + i, 2), y)
        pl.semaphore_signal(barrier, inc=1, device_id=who, device_id_type=MESH)

    loop(1, 2 * plane, 9, greet)
    for step in range(1, ranks):
        pl.semaphore_signal(barrier, inc=1, device_id=peer(step), device_id_type=MESH)

    loads = [
        pltpu.make_async_copy(src, dst, load_sem.at[i])
        for i, (src, dst) in enumerate(
            ((ld_hbm, ld_ref), (dt_hbm, dt_ref), (b_hbm, b_ref), (c_hbm, c_ref))
        )
    ]
    for load in loads:
        load.start()
    for k in range(chunks):
        x_load(k).start()

    @pl.when(core == 0)
    def _():
        sum_in[...] = jnp.zeros_like(sum_in)
        decay_in[...] = jnp.ones_like(decay_in)

    def decay_copy():
        return pltpu.make_async_remote_copy(
            src_ref=rows_e.at[2 * blocks + 1],
            dst_ref=decay_in,
            send_sem=decay_sem.at[0],
            recv_sem=decay_sem.at[1],
            device_id=sibling,
            device_id_type=MESH,
        )

    def sum_copy(k):
        return pltpu.make_async_remote_copy(
            src_ref=summary.at[:, chunk_of(k)],
            dst_ref=sum_in.at[:, chunk_of(k)],
            send_sem=sum_send.at[k],
            recv_sem=sum_recv.at[k],
            device_id=sibling,
            device_id_type=MESH,
        )

    def pass_copy(k):
        return pltpu.make_async_remote_copy(
            src_ref=begin.at[chunk_of(k)],
            dst_ref=begin.at[chunk_of(k)],
            send_sem=pass_send.at[k],
            recv_sem=pass_recv.at[k],
            device_id=sibling,
            device_id_type=MESH,
        )

    def spread_out(k):
        server, half = lax.rem(k, 2), k // 2

        def refs(dz, dx):
            q = dz + 1 + core
            to_x = lax.rem(x + dx, ROW)
            rows = pl.ds(pl.multiple_of(k * CHUNK + (q * ROW + to_x) * piece, piece), piece)
            who = (lax.rem(z + dz + rings, rings) * ROW + to_x, server, y)
            return snap_ref.at[:, rows], spread.at[half, q * ROW + x, pl.ds(2 * core, 2)], who

        def send(src, dst, who):
            pltpu.make_async_remote_copy(
                src_ref=src,
                dst_ref=dst,
                send_sem=spread_send.at[k],
                recv_sem=spread_recv.at[half],
                device_id=who,
                device_id_type=MESH,
            ).start()

        src, dst, who = refs(0, 0)

        @pl.when(core == server)
        def _():
            pltpu.make_async_copy(src, dst, spread_recv.at[half]).start()

        @pl.when(core != server)
        def _():
            send(src, dst, who)

        def one(i):
            dz = (lax.rem(i // ROW + 1, SPAN) - 1) * (1 - 2 * core)
            send(*refs(dz, lax.rem(i, ROW)))

        loop(1, SPAN * ROW, 5, one)

    def slot_of(r):
        return slot_ref[jnp.maximum(first_ref[r] + prefix_ref[r] - 1, 0)]

    def locate(r):
        slot = slot_of(r)
        low = lax.rem(slot, 4)
        q = lax.rem(z - slot // (4 * ROW) + 1 + low // 2 + rings, SPAN)
        place[r] = (q * ROW + lax.rem(slot // 4, ROW)) * 4 + low

    def pick(k):
        server, half = lax.rem(k, 2), k // 2
        here = spread.at[half]
        pltpu.make_async_copy(here, here, spread_recv.at[half]).wait()
        held[...] = here[...].reshape(held.shape)

        def choose(i):
            r = lax.rem(dp + i, plane)
            picked[half, i] = held[place[r]]
            return picked.at[half, i], offered.at[k, z, x], (r, 0, y)

        def send(src, dst, who):
            pltpu.make_async_remote_copy(
                src_ref=src,
                dst_ref=dst,
                send_sem=pick_send.at[half],
                recv_sem=pick_recv.at[k],
                device_id=who,
                device_id_type=MESH,
            ).start()

        loop(1, plane, 5, lambda i: send(*choose(i)))
        src, dst, who = choose(0)

        @pl.when(server == 0)
        def _():
            pltpu.make_async_copy(src, dst, pick_recv.at[k]).start()

        @pl.when(server == 1)
        def _():
            send(src, dst, who)

    def gather(k):
        here = offered.at[k]
        pltpu.make_async_copy(here, here, pick_recv.at[k]).wait()
        came[...] = here[...]
        slot = slot_of(dp)
        low = lax.rem(slot, 4)
        for q in range(SPAN):
            at_z = lax.rem(slot // (4 * ROW) + q - 1 - low // 2 + rings, rings)
            rows = pl.ds(pl.multiple_of(k * CHUNK + q * ROW * piece, ROW * piece), ROW * piece)
            begin[rows, :] = came[at_z].reshape(ROW * piece, STATE)

    def y_copy(k, step):
        cols = chunk_of(k)
        there = pl.ds(pl.multiple_of(y * width + k * CHUNK, CHUNK), CHUNK)
        rows = pl.ds(pl.multiple_of(lax.rem(y + step, ranks) * quarter, quarter), quarter)
        if step == 0:
            return pltpu.make_async_copy(staged.at[rows, cols], o_ref.at[:, there], own_sem.at[k])
        return pltpu.make_async_remote_copy(
            src_ref=staged.at[rows, cols],
            dst_ref=o_ref.at[:, there],
            send_sem=y_send.at[k, step - 1],
            recv_sem=y_recv.at[k, step - 1],
            device_id=peer(step),
            device_id_type=MESH,
        )

    def finish(k):
        @pl.when(core == 0)
        def _():
            gather(k)
            pass_copy(k).start()

        @pl.when(core == 1)
        def _():
            sum_copy(k).wait_recv()
            pass_copy(k).wait_recv()

        cols = chunk_of(k)
        decay = decay_in[0:1, cols]
        earlier = sum_in[:, cols]
        first_state = begin[cols, :]
        for step in (2, 1, 3, 0):
            rows = pl.ds(pl.multiple_of(lax.rem(y + step, ranks) * quarter, quarter), quarter)
            c = c_ref[rows, :]
            mixed = decay * lax.dot_general(
                c, first_state, (((1,), (1,)), ((), ())), preferred_element_type=F32
            ) + jnp.dot(c, earlier, preferred_element_type=F32)
            staged[rows, cols] = (acc[rows, cols] + growth[rows, cols] * mixed).astype(BF16)
            y_copy(k, step).start()

    def stage(s, _):
        @pl.when(s < chunks)
        def _():
            x_load(s).wait()
            local_chunk(
                blocks, s, x_ref, c_ref, sm, bt, run_t, urow, fac, rows_e, state, summary, acc, growth
            )

            @pl.when(core == 0)
            def _():
                sum_copy(s).start()

            @pl.when(lax.rem(s, 2) == core)
            def _():
                pick(s)

        @pl.when(s < chunks - 2)
        def _():
            spread_out(s + 2)

        @pl.when(s >= 1)
        def _():
            finish(s - 1)

        return 0

    pl.semaphore_wait(barrier, 2 * plane - 1 + ranks - 1)
    spread_out(0)
    for load in loads:
        load.wait()
    prepare(blocks, b_ref, c_ref, ld_ref, dt_ref, gain_ref, sm, bt, run_t, urow, fac, rows_e)
    spread_out(1)

    @pl.when(core == 0)
    def _():
        decay_copy().start()

    loop(0, plane, 4, locate)

    @pl.when(core == 1)
    def _():
        decay_copy().wait_recv()

    lax.fori_loop(0, chunks + 1, stage, 0)

    @pl.when(core == 0)
    def _():
        decay_copy().wait_send()

    def drain(k, _):
        for step in range(ranks):
            y_copy(k, step).wait()
        server, half = lax.rem(k, 2), k // 2
        pieces = picked.at[half]

        @pl.when(core == server)
        def _():
            sent = pieces.at[pl.ds(0, plane - 2)]
            pltpu.make_async_copy(sent, sent, spread_send.at[k]).wait()

        @pl.when(core != server)
        def _():
            pltpu.make_async_copy(pieces, pieces, spread_send.at[k]).wait()

        @pl.when(jnp.logical_and(core == 0, server == 0))
        def _():
            sent = pieces.at[pl.ds(0, plane - 1)]
            pltpu.make_async_copy(sent, sent, pick_send.at[half]).wait()

        @pl.when(jnp.logical_and(core == 1, server == 1))
        def _():
            pltpu.make_async_copy(pieces, pieces, pick_send.at[half]).wait()

        @pl.when(core == 0)
        def _():
            sum_copy(k).wait_send()
            pass_copy(k).wait_send()

        return 0

    lax.fori_loop(0, chunks, drain, 0)


def copy_kernel(parts, in_ref, out_ref, held, in_sem, out_sem):
    rows = in_ref.shape[0] // parts

    def part(i):
        return pl.ds(i * rows, rows)

    reads = [
        pltpu.make_async_copy(in_ref.at[part(i)], held.at[part(i)], in_sem.at[i])
        for i in range(parts)
    ]
    writes = [
        pltpu.make_async_copy(held.at[part(i)], out_ref.at[part(i)], out_sem.at[i])
        for i in range(parts)
    ]
    for read in reads:
        read.start()
    for read, write in zip(reads, writes):
        read.wait()
        write.start()
    for write in writes:
        write.wait()


def per_device(
    tokens,
    input_map,
    output_map,
    log_decay,
    step_size,
    skip_gain,
    snapshots,
    first_snap,
    prefix_kilo,
    snap_slot,
):
    length, width = tokens.shape[1:]
    heads = log_decay.shape[1]
    blocks = length // BLOCK
    ranks = lax.axis_size("tensor")
    chunks = width // CHUNK
    out_shape = (length // ranks, width * ranks)
    plane = lax.axis_size("dp")
    piece = CHUNK // (SPAN * ROW)
    hbm, smem = pl.BlockSpec(memory_space=pl.ANY), pl.BlockSpec(memory_space=pltpu.SMEM)
    dma = pltpu.SemaphoreType.DMA
    mixed = pl.pallas_call(
        functools.partial(kernel, blocks, ranks),
        out_shape=jax.ShapeDtypeStruct(out_shape, BF16),
        in_specs=[smem] * 3 + [hbm] * 5 + [pl.BlockSpec(memory_space=pltpu.VMEM), hbm],
        out_specs=hbm,
        scratch_shapes=[
            pltpu.VMEM((length, width), BF16),
            pltpu.VMEM((length, STATE), BF16),
            pltpu.VMEM((length, STATE), BF16),
            pltpu.VMEM((heads, length), F32),
            pltpu.VMEM((heads, length), F32),
            pltpu.VMEM((length, BLOCK), F32),
            pltpu.VMEM((length, BLOCK), F32),
            pltpu.VMEM((length, BLOCK), F32),
            pltpu.VMEM((heads, length), F32),
            pltpu.VMEM((heads, length), F32),
            pltpu.VMEM((2 * blocks + 2, 8, width), F32),
            pltpu.VMEM((STATE, CHUNK), F32),
            pltpu.VMEM((STATE, width), BF16),
            pltpu.VMEM((length, width), F32),
            pltpu.VMEM((length, width), F32),
            pltpu.VMEM((length, width), BF16),
            pltpu.VMEM((STATE, width), BF16),
            pltpu.VMEM((8, width), F32),
            pltpu.VMEM((width, STATE), BF16),
            pltpu.VMEM((chunks // 2, SPAN * ROW, 4, piece, STATE), BF16),
            pltpu.VMEM((SPAN * ROW * 4, piece, STATE), BF16),
            pltpu.VMEM((chunks // 2, plane, piece, STATE), BF16),
            pltpu.VMEM((chunks, plane // ROW, ROW, piece, STATE), BF16),
            pltpu.VMEM((plane // ROW, ROW, piece, STATE), BF16),
            pltpu.SMEM((plane,), jnp.int32),
            dma((4,)),
            dma((chunks,)),
            dma((chunks,)),
            dma((chunks // 2,)),
            dma((chunks // 2,)),
            dma((chunks,)),
            dma((2,)),
            dma((chunks,)),
            dma((chunks,)),
            dma((chunks,)),
            dma((chunks,)),
            dma((chunks, ranks - 1)),
            dma((chunks, ranks - 1)),
            dma((chunks,)),
        ],
        compiler_params=pltpu.CompilerParams(
            collective_id=0, has_side_effects=True, vmem_limit_bytes=56 * 2**20
        ),
        name="scan_and_send",
    )(
        first_snap,
        prefix_kilo,
        snap_slot,
        tokens[0],
        input_map[0],
        output_map[0],
        log_decay[0],
        step_size[0],
        skip_gain.reshape(1, heads),
        snapshots.reshape(snapshots.shape[0], width, STATE),
    )
    parts = 4
    result = pl.pallas_call(
        functools.partial(copy_kernel, parts),
        out_shape=jax.ShapeDtypeStruct(out_shape, BF16),
        in_specs=[pl.BlockSpec(memory_space=pl.ANY)],
        out_specs=pl.BlockSpec(memory_space=pl.ANY),
        scratch_shapes=[
            pltpu.VMEM(out_shape, BF16),
            pltpu.SemaphoreType.DMA((parts,)),
            pltpu.SemaphoreType.DMA((parts,)),
        ],
        compiler_params=pltpu.CompilerParams(vmem_limit_bytes=60 * 2**20),
        name="place_result",
    )(mixed)
    return result[None]


def solution(mesh):
    placed = (
        P("dp", "seq", "tensor"),
        P("dp", "seq", "tensor"),
        P("dp", "seq", "tensor"),
        P("dp", "tensor", "seq"),
        P("dp", "tensor", "seq"),
        P("tensor"),
        P(("dp", "seq"), "tensor", None, None),
        P(),
        P(),
        P(),
    )
    return jax.shard_map(
        per_device,
        mesh=mesh,
        in_specs=placed,
        out_specs=P("dp", ("seq", "tensor"), None),
        check_vma=False,
    )
```

```python
import functools

import jax
import jax.numpy as jnp
from jax import lax
from jax.experimental import pallas as pl
from jax.experimental.pallas import tpu as pltpu
from jax.sharding import PartitionSpec as P

HEAD_DIM = 64
STATE = 128
BLOCK = 128
CHUNK = 8 * HEAD_DIM
LOG2E = 1.4426950408889634
ROW = 4
SPAN = 4
MESH = pl.DeviceIdType.MESH
F32 = jnp.float32
BF16 = jnp.bfloat16


def prepare(
    blocks, b_ref, c_ref, ld_ref, dt_ref, gain_ref, sm, bt, run_t, urow, fac, rows_e, reached
):
    heads = ld_ref.shape[0]
    width = heads * HEAD_DIM
    row = lax.broadcasted_iota(jnp.int32, (BLOCK, BLOCK), 0)
    col = lax.broadcasted_iota(jnp.int32, (BLOCK, BLOCK), 1)
    upto = (row <= col).astype(F32)
    ends = []
    so_far = jnp.zeros((heads, 1), F32)
    for b in range(blocks):
        at = pl.ds(b * BLOCK, BLOCK)
        run = jnp.dot(
            ld_ref[:, at], upto, precision=lax.Precision.HIGHEST, preferred_element_type=F32
        )
        run = run * LOG2E
        step = dt_ref[:, at]
        end = run[:, BLOCK - 1 :]
        urow[:, at] = run - jnp.log2(step)
        fac[:, at] = jnp.exp2(end - run) * step
        reached[:, at] = jnp.exp2(run + so_far)
        so_far = so_far + end
        padded = jnp.concatenate([run, jnp.zeros((BLOCK - heads, BLOCK), F32)], axis=0)
        turned = padded.T
        run_t[at, :] = turned
        ends.append(turned[BLOCK - 1 :, :])
        inputs = b_ref[at, :]
        scores = lax.dot_general(
            c_ref[at, :], inputs, (((1,), (1,)), ((), ())), preferred_element_type=F32
        )
        sm[at, :] = jnp.where(row >= col, scores, 0.0)
        bt[at, :] = inputs.astype(F32).T
    stacked = jnp.concatenate(ends, axis=0)
    pad = (-stacked.shape[0]) % 8
    if pad:
        stacked = jnp.concatenate([stacked, jnp.zeros((pad, BLOCK), F32)], axis=0)
    spot = lax.broadcasted_iota(jnp.int32, (BLOCK, width), 0)
    head = lax.broadcasted_iota(jnp.int32, (BLOCK, width), 1) // HEAD_DIM
    spread = (spot == head).astype(F32)
    wide = jnp.dot(stacked, spread, precision=lax.Precision.HIGHEST, preferred_element_type=F32)
    gain = jnp.dot(
        gain_ref[...], spread[:heads], precision=lax.Precision.HIGHEST, preferred_element_type=F32
    )
    reach = jnp.zeros((1, width), F32)
    for b in range(blocks):
        end = wide[b : b + 1, :]
        rows_e[b] = jnp.broadcast_to(jnp.exp2(end), (8, width))
        rows_e[blocks + 1 + b] = jnp.broadcast_to(jnp.exp2(reach), (8, width))
        reach = reach + end
    rows_e[blocks] = jnp.broadcast_to(gain, (8, width))
    rows_e[2 * blocks + 1] = jnp.broadcast_to(jnp.exp2(reach), (8, width))


def local_chunk(
    blocks, k, x_ref, c_ref, sm, bt, run_t, urow, fac, rows_e, state, summary, acc, growth
):
    cols = pl.ds(pl.multiple_of(k * CHUNK, CHUNK), CHUNK)
    octet = pl.ds(pl.multiple_of(k * 8, 8), 8)
    pair_width = 2 * HEAD_DIM
    first = lax.broadcasted_iota(jnp.int32, (1, pair_width), 1) < HEAD_DIM
    keep0 = jnp.where(first, 1.0, 0.0).astype(BF16)
    keep1 = jnp.where(first, 0.0, 1.0).astype(BF16)
    state[...] = jnp.zeros_like(state)

    def one(b, _):
        at = pl.ds(pl.multiple_of(b * BLOCK, BLOCK), BLOCK)
        turned = pltpu.roll(run_t[at, :], lax.rem(BLOCK - 8 * k, BLOCK), 1)
        u = urow[octet, at]
        f = fac[octet, at]
        carried = jnp.dot(c_ref[at, :], state[...].astype(BF16), preferred_element_type=F32)
        for j in range(CHUNK // pair_width):
            mine = slice(j * pair_width, (j + 1) * pair_width)
            here = pl.ds(pl.multiple_of(k * CHUNK + j * pair_width, pair_width), pair_width)
            h0, h1 = slice(2 * j, 2 * j + 1), slice(2 * j + 1, 2 * j + 2)
            scores = sm[at, :]
            back = bt[at, :]
            run0 = jnp.broadcast_to(turned[:, h0], (BLOCK, BLOCK))
            run1 = jnp.broadcast_to(turned[:, h1], (BLOCK, BLOCK))
            w0 = (scores * jnp.exp2(jnp.minimum(run0 - u[h0], 64.0))).astype(BF16)
            w1 = (scores * jnp.exp2(jnp.minimum(run1 - u[h1], 64.0))).astype(BF16)
            b0 = (back * f[h0]).astype(BF16)
            b1 = (back * f[h1]).astype(BF16)
            x = x_ref[at, here]
            left = jnp.concatenate(
                [jnp.concatenate([w0, w1], axis=1), jnp.concatenate([b0, b1], axis=1)], axis=0
            )
            right = jnp.concatenate([x * keep0, x * keep1], axis=0)
            both = jnp.dot(left, right, preferred_element_type=F32)
            grown = jnp.exp2(jnp.where(first, run0, run1))
            acc[at, here] = (
                both[:BLOCK]
                + grown * carried[:, mine]
                + x.astype(F32) * rows_e[blocks, :, here][0:1, :]
            )
            growth[at, here] = grown * rows_e[blocks + 1 + b, :, here][0:1, :]
            state[:, mine] = rows_e[b, :, here][0:1, :] * state[:, mine] + both[BLOCK:]
        return 0

    lax.fori_loop(0, blocks, one, 0, unroll=2)
    summary[:, cols] = state[...].astype(BF16)


def loop(start, stop, group, body):
    def step(j, _):
        for i in range(group):
            body(start + j * group + i)
        return 0

    steps = (stop - start) // group
    lax.fori_loop(0, steps, step, 0)
    for i in range(start + steps * group, stop):
        body(i)


def kernel(
    blocks,
    ranks,
    first_ref,
    prefix_ref,
    slot_ref,
    x_hbm,
    b_hbm,
    c_hbm,
    ld_hbm,
    dt_hbm,
    gain_ref,
    snap_ref,
    o_ref,
    x_ref,
    b_ref,
    c_ref,
    ld_ref,
    dt_ref,
    sm,
    bt,
    run_t,
    urow,
    fac,
    rows_e,
    state,
    summary,
    acc,
    growth,
    staged,
    sum_in,
    decay_in,
    begin,
    spread,
    held,
    picked,
    offered,
    came,
    place,
    reached,
    entering,
    early,
    c_in,
    decays_in,
    state_in,
    load_sem,
    x_sem,
    spread_send,
    spread_recv,
    pick_send,
    pick_recv,
    decay_sem,
    sum_send,
    sum_recv,
    pass_send,
    pass_recv,
    y_send,
    y_recv,
    own_sem,
    map_send,
    map_recv,
    early_send,
    early_recv,
    state_send,
    state_recv,
    late_sem,
):
    dp, core, y = lax.axis_index("dp"), lax.axis_index("seq"), lax.axis_index("tensor")
    z, x = dp // ROW, dp % ROW
    plane = lax.axis_size("dp")
    rings = plane // ROW
    sibling = (dp, 1 - core, y)
    quarter = blocks * BLOCK // ranks
    width = x_ref.shape[1]
    chunks = width // CHUNK
    ahead = early.shape[0]
    piece = CHUNK // (SPAN * ROW)

    def peer(step):
        return (dp, core, lax.rem(y + step, ranks))

    def chunk_of(k):
        return pl.ds(pl.multiple_of(k * CHUNK, CHUNK), CHUNK)

    def x_load(k):
        cols = chunk_of(k)
        return pltpu.make_async_copy(x_hbm.at[:, cols], x_ref.at[:, cols], x_sem.at[k])

    barrier = pltpu.get_barrier_semaphore()

    def greet(i):
        who = (lax.rem(dp + i // 2, plane), lax.rem(core + i, 2), y)
        pl.semaphore_signal(barrier, inc=1, device_id=who, device_id_type=MESH)

    loop(1, 2 * plane, 9, greet)
    for step in range(1, ranks):
        pl.semaphore_signal(barrier, inc=1, device_id=peer(step), device_id_type=MESH)

    loads = [
        pltpu.make_async_copy(src, dst, load_sem.at[i])
        for i, (src, dst) in enumerate(
            ((ld_hbm, ld_ref), (dt_hbm, dt_ref), (b_hbm, b_ref), (c_hbm, c_ref))
        )
    ]
    for load in loads:
        load.start()
    for k in range(chunks):
        x_load(k).start()

    @pl.when(core == 0)
    def _():
        sum_in[...] = jnp.zeros_like(sum_in)
        decay_in[...] = jnp.ones_like(decay_in)

    def decay_copy():
        return pltpu.make_async_remote_copy(
            src_ref=rows_e.at[2 * blocks + 1],
            dst_ref=decay_in,
            send_sem=decay_sem.at[0],
            recv_sem=decay_sem.at[1],
            device_id=sibling,
            device_id_type=MESH,
        )

    def sum_copy(k):
        return pltpu.make_async_remote_copy(
            src_ref=summary.at[:, chunk_of(k)],
            dst_ref=sum_in.at[:, chunk_of(k)],
            send_sem=sum_send.at[k],
            recv_sem=sum_recv.at[k],
            device_id=sibling,
            device_id_type=MESH,
        )

    def pass_copy(k):
        return pltpu.make_async_remote_copy(
            src_ref=begin.at[chunk_of(k)],
            dst_ref=begin.at[chunk_of(k)],
            send_sem=pass_send.at[k],
            recv_sem=pass_recv.at[k],
            device_id=sibling,
            device_id_type=MESH,
        )

    def spread_out(k):
        server, half = lax.rem(k, 2), k // 2

        def refs(dz, dx):
            q = dz + 1 + core
            to_x = lax.rem(x + dx, ROW)
            rows = pl.ds(pl.multiple_of(k * CHUNK + (q * ROW + to_x) * piece, piece), piece)
            who = (lax.rem(z + dz + rings, rings) * ROW + to_x, server, y)
            return snap_ref.at[:, rows], spread.at[half, q * ROW + x, pl.ds(2 * core, 2)], who

        def send(src, dst, who):
            pltpu.make_async_remote_copy(
                src_ref=src,
                dst_ref=dst,
                send_sem=spread_send.at[k],
                recv_sem=spread_recv.at[half],
                device_id=who,
                device_id_type=MESH,
            ).start()

        src, dst, who = refs(0, 0)

        @pl.when(core == server)
        def _():
            pltpu.make_async_copy(src, dst, spread_recv.at[half]).start()

        @pl.when(core != server)
        def _():
            send(src, dst, who)

        def one(i):
            dz = (lax.rem(i // ROW + 1, SPAN) - 1) * (1 - 2 * core)
            send(*refs(dz, lax.rem(i, ROW)))

        loop(1, SPAN * ROW, 5, one)

    def slot_of(r):
        return slot_ref[jnp.maximum(first_ref[r] + prefix_ref[r] - 1, 0)]

    def locate(r):
        slot = slot_of(r)
        low = lax.rem(slot, 4)
        q = lax.rem(z - slot // (4 * ROW) + 1 + low // 2 + rings, SPAN)
        place[r] = (q * ROW + lax.rem(slot // 4, ROW)) * 4 + low

    def pick(k):
        server, half = lax.rem(k, 2), k // 2
        here = spread.at[half]
        pltpu.make_async_copy(here, here, spread_recv.at[half]).wait()
        held[...] = here[...].reshape(held.shape)

        def choose(i):
            r = lax.rem(dp + i, plane)
            picked[half, i] = held[place[r]]
            return picked.at[half, i], offered.at[k, z, x], (r, 0, y)

        def send(src, dst, who):
            pltpu.make_async_remote_copy(
                src_ref=src,
                dst_ref=dst,
                send_sem=pick_send.at[half],
                recv_sem=pick_recv.at[k],
                device_id=who,
                device_id_type=MESH,
            ).start()

        loop(1, plane, 5, lambda i: send(*choose(i)))
        src, dst, who = choose(0)

        @pl.when(server == 0)
        def _():
            pltpu.make_async_copy(src, dst, pick_recv.at[k]).start()

        @pl.when(server == 1)
        def _():
            send(src, dst, who)

    def gather(k):
        here = offered.at[k]
        pltpu.make_async_copy(here, here, pick_recv.at[k]).wait()
        came[...] = here[...]
        slot = slot_of(dp)
        low = lax.rem(slot, 4)
        for q in range(SPAN):
            at_z = lax.rem(slot // (4 * ROW) + q - 1 - low // 2 + rings, rings)
            rows = pl.ds(pl.multiple_of(k * CHUNK + q * ROW * piece, ROW * piece), ROW * piece)
            begin[rows, :] = came[at_z].reshape(ROW * piece, STATE)

    def y_copy(k, step):
        cols = chunk_of(k)
        there = pl.ds(pl.multiple_of(y * width + k * CHUNK, CHUNK), CHUNK)
        rows = pl.ds(pl.multiple_of(lax.rem(y + step, ranks) * quarter, quarter), quarter)
        if step == 0:
            return pltpu.make_async_copy(staged.at[rows, cols], o_ref.at[:, there], own_sem.at[k])
        return pltpu.make_async_remote_copy(
            src_ref=staged.at[rows, cols],
            dst_ref=o_ref.at[:, there],
            send_sem=y_send.at[k, step - 1],
            recv_sem=y_recv.at[k, step - 1],
            device_id=peer(step),
            device_id_type=MESH,
        )

    def map_copies(step):
        rows = pl.ds(pl.multiple_of(lax.rem(y + step, ranks) * quarter, quarter), quarter)
        pairs = ((c_ref.at[rows], c_in), (reached.at[pl.ds(0, ahead * 8), rows], decays_in))
        return [
            pltpu.make_async_remote_copy(
                src_ref=src,
                dst_ref=dst.at[step - 1],
                send_sem=map_send.at[step - 1, i],
                recv_sem=map_recv.at[step - 1, i],
                device_id=peer(step),
                device_id_type=MESH,
            )
            for i, (src, dst) in enumerate(pairs)
        ]

    def early_copy(k, step):
        rows = pl.ds(pl.multiple_of(lax.rem(y + step, ranks) * quarter, quarter), quarter)
        return pltpu.make_async_remote_copy(
            src_ref=staged.at[rows, chunk_of(k)],
            dst_ref=early.at[k, step - 1],
            send_sem=early_send.at[k, step - 1],
            recv_sem=early_recv.at[k, step - 1],
            device_id=peer(step),
            device_id_type=MESH,
        )

    def state_copy(k, step):
        return pltpu.make_async_remote_copy(
            src_ref=entering.at[:, chunk_of(k)],
            dst_ref=state_in.at[k, step - 1],
            send_sem=state_send.at[k, step - 1],
            recv_sem=state_recv.at[k, step - 1],
            device_id=peer(step),
            device_id_type=MESH,
        )

    def late_copy(k, step):
        whose = lax.rem(y + ranks - step, ranks)
        there = pl.ds(pl.multiple_of(whose * width + k * CHUNK, CHUNK), CHUNK)
        return pltpu.make_async_copy(
            early.at[k, step - 1], o_ref.at[:, there], late_sem.at[k, step - 1]
        )

    def send_early(k):
        cols = chunk_of(k)
        for step in (2, 1, 3):
            rows = pl.ds(pl.multiple_of(lax.rem(y + step, ranks) * quarter, quarter), quarter)
            staged[rows, cols] = acc[rows, cols].astype(BF16)
            early_copy(k, step).start()

    def finish_late(k):
        spot = lax.broadcasted_iota(jnp.int32, (BLOCK, CHUNK), 0)
        head = lax.broadcasted_iota(jnp.int32, (BLOCK, CHUNK), 1) // HEAD_DIM + 8 * k
        widen = (spot == head).astype(F32)
        for step in (1, 3, 2):
            early_copy(k, step).wait_recv()
            state_copy(k, step).wait_recv()
            entered = state_in[k, step - 1]
            for half in range(quarter // BLOCK):
                at = pl.ds(half * BLOCK, BLOCK)
                decays = decays_in[step - 1, :, at]
                padded = jnp.concatenate(
                    [decays, jnp.zeros((BLOCK - decays.shape[0], BLOCK), F32)], axis=0
                )
                grown = jnp.dot(
                    padded.T,
                    widen,
                    precision=lax.Precision.HIGHEST,
                    preferred_element_type=F32,
                )
                mixed = jnp.dot(c_in[step - 1, at, :], entered, preferred_element_type=F32)
                early[k, step - 1, at, :] = (
                    early[k, step - 1, at, :].astype(F32) + grown * mixed
                ).astype(BF16)
            late_copy(k, step).start()

    def finish(k):
        @pl.when(core == 0)
        def _():
            gather(k)
            pass_copy(k).start()

        @pl.when(core == 1)
        def _():
            sum_copy(k).wait_recv()
            pass_copy(k).wait_recv()

        cols = chunk_of(k)
        for i in range(CHUNK // STATE):
            part = pl.ds(pl.multiple_of(k * CHUNK + i * STATE, STATE), STATE)
            loaded = begin[part, :].astype(F32).T
            entering[:, part] = (
                decay_in[0:1, part] * loaded + sum_in[:, part].astype(F32)
            ).astype(BF16)
        entered = entering[:, cols]

        def output(step):
            rows = pl.ds(pl.multiple_of(lax.rem(y + step, ranks) * quarter, quarter), quarter)
            mixed = jnp.dot(c_ref[rows, :], entered, preferred_element_type=F32)
            staged[rows, cols] = (acc[rows, cols] + growth[rows, cols] * mixed).astype(BF16)
            y_copy(k, step).start()

        @pl.when(k < ahead)
        def _():
            for step in (2, 1, 3):
                state_copy(k, step).start()

        @pl.when(k >= ahead)
        def _():
            for step in (2, 1, 3):
                output(step)

        output(0)

    def stage(s, _):
        @pl.when(s < chunks)
        def _():
            x_load(s).wait()
            local_chunk(
                blocks, s, x_ref, c_ref, sm, bt, run_t, urow, fac, rows_e, state, summary, acc, growth
            )

            @pl.when(s < ahead)
            def _():
                send_early(s)

            @pl.when(s == 0)
            def _():
                for step in (2, 1, 3):
                    for copy in map_copies(step):
                        copy.start()
                spread_out(1)
                loop(0, plane, 4, locate)

                @pl.when(core == 1)
                def _():
                    decay_copy().wait_recv()

            @pl.when(core == 0)
            def _():
                sum_copy(s).start()

            @pl.when(lax.rem(s, 2) == core)
            def _():
                pick(s)

        @pl.when(s < chunks - 2)
        def _():
            spread_out(s + 2)

        @pl.when(s >= 1)
        def _():
            finish(s - 1)

        return 0

    for load in loads:
        load.wait()
    prepare(
        blocks, b_ref, c_ref, ld_ref, dt_ref, gain_ref, sm, bt, run_t, urow, fac, rows_e, reached
    )
    pl.semaphore_wait(barrier, 2 * plane - 1 + ranks - 1)
    spread_out(0)

    @pl.when(core == 0)
    def _():
        decay_copy().start()

    lax.fori_loop(0, chunks + 1, stage, 0)
    for step in (1, 3, 2):
        for copy in map_copies(step):
            copy.wait()

    def late(k, _):
        finish_late(k)
        return 0

    lax.fori_loop(0, ahead, late, 0)

    @pl.when(core == 0)
    def _():
        decay_copy().wait_send()

    def drain(k, _):
        y_copy(k, 0).wait()

        @pl.when(k < ahead)
        def _():
            for step in range(1, ranks):
                early_copy(k, step).wait_send()
                state_copy(k, step).wait_send()
                late_copy(k, step).wait()

        @pl.when(k >= ahead)
        def _():
            for step in range(1, ranks):
                y_copy(k, step).wait()

        server, half = lax.rem(k, 2), k // 2
        pieces = picked.at[half]

        @pl.when(core == server)
        def _():
            sent = pieces.at[pl.ds(0, plane - 2)]
            pltpu.make_async_copy(sent, sent, spread_send.at[k]).wait()

        @pl.when(core != server)
        def _():
            pltpu.make_async_copy(pieces, pieces, spread_send.at[k]).wait()

        @pl.when(jnp.logical_and(core == 0, server == 0))
        def _():
            sent = pieces.at[pl.ds(0, plane - 1)]
            pltpu.make_async_copy(sent, sent, pick_send.at[half]).wait()

        @pl.when(jnp.logical_and(core == 1, server == 1))
        def _():
            pltpu.make_async_copy(pieces, pieces, pick_send.at[half]).wait()

        @pl.when(core == 0)
        def _():
            sum_copy(k).wait_send()
            pass_copy(k).wait_send()

        return 0

    lax.fori_loop(0, chunks, drain, 0)


def copy_kernel(parts, in_ref, out_ref, held, in_sem, out_sem):
    rows = in_ref.shape[0] // parts

    def part(i):
        return pl.ds(i * rows, rows)

    reads = [
        pltpu.make_async_copy(in_ref.at[part(i)], held.at[part(i)], in_sem.at[i])
        for i in range(parts)
    ]
    writes = [
        pltpu.make_async_copy(held.at[part(i)], out_ref.at[part(i)], out_sem.at[i])
        for i in range(parts)
    ]
    for read in reads:
        read.start()
    for read, write in zip(reads, writes):
        read.wait()
        write.start()
    for write in writes:
        write.wait()


def per_device(
    tokens,
    input_map,
    output_map,
    log_decay,
    step_size,
    skip_gain,
    snapshots,
    first_snap,
    prefix_kilo,
    snap_slot,
):
    length, width = tokens.shape[1:]
    heads = log_decay.shape[1]
    blocks = length // BLOCK
    ranks = lax.axis_size("tensor")
    chunks = width // CHUNK
    out_shape = (length // ranks, width * ranks)
    plane = lax.axis_size("dp")
    piece = CHUNK // (SPAN * ROW)
    ahead = 1
    hbm, smem = pl.BlockSpec(memory_space=pl.ANY), pl.BlockSpec(memory_space=pltpu.SMEM)
    dma = pltpu.SemaphoreType.DMA
    mixed = pl.pallas_call(
        functools.partial(kernel, blocks, ranks),
        out_shape=jax.ShapeDtypeStruct(out_shape, BF16),
        in_specs=[smem] * 3 + [hbm] * 5 + [pl.BlockSpec(memory_space=pltpu.VMEM), hbm],
        out_specs=hbm,
        scratch_shapes=[
            pltpu.VMEM((length, width), BF16),
            pltpu.VMEM((length, STATE), BF16),
            pltpu.VMEM((length, STATE), BF16),
            pltpu.VMEM((heads, length), F32),
            pltpu.VMEM((heads, length), F32),
            pltpu.VMEM((length, BLOCK), F32),
            pltpu.VMEM((length, BLOCK), F32),
            pltpu.VMEM((length, BLOCK), F32),
            pltpu.VMEM((heads, length), F32),
            pltpu.VMEM((heads, length), F32),
            pltpu.VMEM((2 * blocks + 2, 8, width), F32),
            pltpu.VMEM((STATE, CHUNK), F32),
            pltpu.VMEM((STATE, width), BF16),
            pltpu.VMEM((length, width), F32),
            pltpu.VMEM((length, width), F32),
            pltpu.VMEM((length, width), BF16),
            pltpu.VMEM((STATE, width), BF16),
            pltpu.VMEM((8, width), F32),
            pltpu.VMEM((width, STATE), BF16),
            pltpu.VMEM((chunks // 2, SPAN * ROW, 4, piece, STATE), BF16),
            pltpu.VMEM((SPAN * ROW * 4, piece, STATE), BF16),
            pltpu.VMEM((chunks // 2, plane, piece, STATE), BF16),
            pltpu.VMEM((chunks, plane // ROW, ROW, piece, STATE), BF16),
            pltpu.VMEM((plane // ROW, ROW, piece, STATE), BF16),
            pltpu.SMEM((plane,), jnp.int32),
            pltpu.VMEM((heads, length), F32),
            pltpu.VMEM((STATE, width), BF16),
            pltpu.VMEM((ahead, ranks - 1, length // ranks, CHUNK), BF16),
            pltpu.VMEM((ranks - 1, length // ranks, STATE), BF16),
            pltpu.VMEM((ranks - 1, ahead * 8, length // ranks), F32),
            pltpu.VMEM((ahead, ranks - 1, STATE, CHUNK), BF16),
            dma((4,)),
            dma((chunks,)),
            dma((chunks,)),
            dma((chunks // 2,)),
            dma((chunks // 2,)),
            dma((chunks,)),
            dma((2,)),
            dma((chunks,)),
            dma((chunks,)),
            dma((chunks,)),
            dma((chunks,)),
            dma((chunks, ranks - 1)),
            dma((chunks, ranks - 1)),
            dma((chunks,)),
            dma((ranks - 1, 2)),
            dma((ranks - 1, 2)),
            dma((ahead, ranks - 1)),
            dma((ahead, ranks - 1)),
            dma((ahead, ranks - 1)),
            dma((ahead, ranks - 1)),
            dma((ahead, ranks - 1)),
        ],
        compiler_params=pltpu.CompilerParams(
            collective_id=0, has_side_effects=True, vmem_limit_bytes=56 * 2**20
        ),
        name="scan_and_send",
    )(
        first_snap,
        prefix_kilo,
        snap_slot,
        tokens[0],
        input_map[0],
        output_map[0],
        log_decay[0],
        step_size[0],
        skip_gain.reshape(1, heads),
        snapshots.reshape(snapshots.shape[0], width, STATE),
    )
    parts = 4
    result = pl.pallas_call(
        functools.partial(copy_kernel, parts),
        out_shape=jax.ShapeDtypeStruct(out_shape, BF16),
        in_specs=[pl.BlockSpec(memory_space=pl.ANY)],
        out_specs=pl.BlockSpec(memory_space=pl.ANY),
        scratch_shapes=[
            pltpu.VMEM(out_shape, BF16),
            pltpu.SemaphoreType.DMA((parts,)),
            pltpu.SemaphoreType.DMA((parts,)),
        ],
        compiler_params=pltpu.CompilerParams(vmem_limit_bytes=60 * 2**20),
        name="place_result",
    )(mixed)
    return result[None]


def solution(mesh):
    placed = (
        P("dp", "seq", "tensor"),
        P("dp", "seq", "tensor"),
        P("dp", "seq", "tensor"),
        P("dp", "tensor", "seq"),
        P("dp", "tensor", "seq"),
        P("tensor"),
        P(("dp", "seq"), "tensor", None, None),
        P(),
        P(),
        P(),
    )
    return jax.shard_map(
        per_device,
        mesh=mesh,
        in_specs=placed,
        out_specs=P("dp", ("seq", "tensor"), None),
        check_vma=False,
    )
```

```python
import functools

import jax
import jax.numpy as jnp
from jax import lax
from jax.experimental import pallas as pl
from jax.experimental.pallas import tpu as pltpu
from jax.sharding import PartitionSpec as P

HEAD_DIM = 64
STATE = 128
BLOCK = 128
CHUNK = 8 * HEAD_DIM
LOG2E = 1.4426950408889634
ROW = 4
SPAN = 4
EARLY = 1
MESH = pl.DeviceIdType.MESH
F32 = jnp.float32
BF16 = jnp.bfloat16


def prepare(
    blocks, b_ref, c_ref, ld_ref, dt_ref, gain_ref, sm, bt, run_t, urow, fac, rows_e, reached
):
    heads = ld_ref.shape[0]
    width = heads * HEAD_DIM
    row = lax.broadcasted_iota(jnp.int32, (BLOCK, BLOCK), 0)
    col = lax.broadcasted_iota(jnp.int32, (BLOCK, BLOCK), 1)
    upto = (row <= col).astype(F32)
    ends = []
    so_far = jnp.zeros((heads, 1), F32)
    for b in range(blocks):
        at = pl.ds(b * BLOCK, BLOCK)
        run = jnp.dot(
            ld_ref[:, at], upto, precision=lax.Precision.HIGHEST, preferred_element_type=F32
        )
        run = run * LOG2E
        step = dt_ref[:, at]
        end = run[:, BLOCK - 1 :]
        urow[:, at] = run - jnp.log2(step)
        fac[:, at] = jnp.exp2(end - run) * step
        reached[:, at] = jnp.exp2(run + so_far)
        so_far = so_far + end
        padded = jnp.concatenate([run, jnp.zeros((BLOCK - heads, BLOCK), F32)], axis=0)
        turned = padded.T
        run_t[at, :] = turned
        ends.append(turned[BLOCK - 1 :, :])
        inputs = b_ref[at, :]
        scores = lax.dot_general(
            c_ref[at, :], inputs, (((1,), (1,)), ((), ())), preferred_element_type=F32
        )
        sm[at, :] = jnp.where(row >= col, scores, 0.0)
        bt[at, :] = inputs.astype(F32).T
    stacked = jnp.concatenate(ends, axis=0)
    pad = (-stacked.shape[0]) % 8
    if pad:
        stacked = jnp.concatenate([stacked, jnp.zeros((pad, BLOCK), F32)], axis=0)
    spot = lax.broadcasted_iota(jnp.int32, (BLOCK, width), 0)
    head = lax.broadcasted_iota(jnp.int32, (BLOCK, width), 1) // HEAD_DIM
    spread = (spot == head).astype(F32)
    wide = jnp.dot(stacked, spread, precision=lax.Precision.HIGHEST, preferred_element_type=F32)
    gain = jnp.dot(
        gain_ref[...], spread[:heads], precision=lax.Precision.HIGHEST, preferred_element_type=F32
    )
    reach = jnp.zeros((1, width), F32)
    for b in range(blocks):
        end = wide[b : b + 1, :]
        rows_e[b] = jnp.broadcast_to(jnp.exp2(end), (8, width))
        rows_e[blocks + 1 + b] = jnp.broadcast_to(jnp.exp2(reach), (8, width))
        reach = reach + end
    rows_e[blocks] = jnp.broadcast_to(gain, (8, width))
    rows_e[2 * blocks + 1] = jnp.broadcast_to(jnp.exp2(reach), (8, width))


def local_chunk(
    blocks, k, x_ref, c_ref, sm, bt, run_t, urow, fac, rows_e, state, summary, acc, growth
):
    cols = pl.ds(pl.multiple_of(k * CHUNK, CHUNK), CHUNK)
    octet = pl.ds(pl.multiple_of(k * 8, 8), 8)
    pair_width = 2 * HEAD_DIM
    first = lax.broadcasted_iota(jnp.int32, (1, pair_width), 1) < HEAD_DIM
    keep0 = jnp.where(first, 1.0, 0.0).astype(BF16)
    keep1 = jnp.where(first, 0.0, 1.0).astype(BF16)
    state[...] = jnp.zeros_like(state)

    def one(b, _):
        at = pl.ds(pl.multiple_of(b * BLOCK, BLOCK), BLOCK)
        turned = pltpu.roll(run_t[at, :], lax.rem(BLOCK - 8 * k, BLOCK), 1)
        u = urow[octet, at]
        f = fac[octet, at]
        carried = jnp.dot(c_ref[at, :], state[...].astype(BF16), preferred_element_type=F32)
        for j in range(CHUNK // pair_width):
            mine = slice(j * pair_width, (j + 1) * pair_width)
            here = pl.ds(pl.multiple_of(k * CHUNK + j * pair_width, pair_width), pair_width)
            h0, h1 = slice(2 * j, 2 * j + 1), slice(2 * j + 1, 2 * j + 2)
            scores = sm[at, :]
            back = bt[at, :]
            run0 = jnp.broadcast_to(turned[:, h0], (BLOCK, BLOCK))
            run1 = jnp.broadcast_to(turned[:, h1], (BLOCK, BLOCK))
            w0 = (scores * jnp.exp2(jnp.minimum(run0 - u[h0], 64.0))).astype(BF16)
            w1 = (scores * jnp.exp2(jnp.minimum(run1 - u[h1], 64.0))).astype(BF16)
            b0 = (back * f[h0]).astype(BF16)
            b1 = (back * f[h1]).astype(BF16)
            x = x_ref[at, here]
            left = jnp.concatenate(
                [jnp.concatenate([w0, w1], axis=1), jnp.concatenate([b0, b1], axis=1)], axis=0
            )
            right = jnp.concatenate([x * keep0, x * keep1], axis=0)
            both = jnp.dot(left, right, preferred_element_type=F32)
            grown = jnp.exp2(jnp.where(first, run0, run1))
            acc[at, here] = (
                both[:BLOCK]
                + grown * carried[:, mine]
                + x.astype(F32) * rows_e[blocks, :, here][0:1, :]
            )
            growth[at, here] = grown * rows_e[blocks + 1 + b, :, here][0:1, :]
            state[:, mine] = rows_e[b, :, here][0:1, :] * state[:, mine] + both[BLOCK:]
        return 0

    lax.fori_loop(0, blocks, one, 0, unroll=2)
    summary[:, cols] = state[...].astype(BF16)


def loop(start, stop, group, body):
    def step(j, _):
        for i in range(group):
            body(start + j * group + i)
        return 0

    steps = (stop - start) // group
    lax.fori_loop(0, steps, step, 0)
    for i in range(start + steps * group, stop):
        body(i)


def kernel(
    blocks,
    ranks,
    first_ref,
    prefix_ref,
    slot_ref,
    x_hbm,
    b_hbm,
    c_hbm,
    ld_hbm,
    dt_hbm,
    gain_ref,
    snap_ref,
    o_ref,
    x_ref,
    b_ref,
    c_ref,
    ld_ref,
    dt_ref,
    sm,
    bt,
    run_t,
    urow,
    fac,
    rows_e,
    state,
    summary,
    acc,
    growth,
    staged,
    sum_in,
    decay_in,
    begin,
    spread,
    held,
    picked,
    offered,
    came,
    place,
    reached,
    entering,
    early,
    c_in,
    decays_in,
    state_in,
    load_sem,
    x_sem,
    spread_send,
    spread_recv,
    pick_send,
    pick_recv,
    decay_sem,
    sum_send,
    sum_recv,
    pass_send,
    pass_recv,
    y_send,
    y_recv,
    own_sem,
    map_send,
    map_recv,
    early_send,
    early_recv,
    state_send,
    state_recv,
    late_sem,
):
    dp, core, y = lax.axis_index("dp"), lax.axis_index("seq"), lax.axis_index("tensor")
    z, x = dp // ROW, dp % ROW
    plane = lax.axis_size("dp")
    rings = plane // ROW
    sibling = (dp, 1 - core, y)
    quarter = blocks * BLOCK // ranks
    width = x_ref.shape[1]
    chunks = width // CHUNK
    piece = CHUNK // (SPAN * ROW)

    def peer(step):
        return (dp, core, lax.rem(y + step, ranks))

    def chunk_of(k):
        return pl.ds(pl.multiple_of(k * CHUNK, CHUNK), CHUNK)

    def x_load(k):
        cols = chunk_of(k)
        return pltpu.make_async_copy(x_hbm.at[:, cols], x_ref.at[:, cols], x_sem.at[k])

    barrier = pltpu.get_barrier_semaphore()

    def greet(i):
        who = (lax.rem(dp + i // 2, plane), lax.rem(core + i, 2), y)
        pl.semaphore_signal(barrier, inc=1, device_id=who, device_id_type=MESH)

    loop(1, 2 * plane, 9, greet)
    for step in range(1, ranks):
        pl.semaphore_signal(barrier, inc=1, device_id=peer(step), device_id_type=MESH)

    loads = [
        pltpu.make_async_copy(src, dst, load_sem.at[i])
        for i, (src, dst) in enumerate(
            ((ld_hbm, ld_ref), (dt_hbm, dt_ref), (b_hbm, b_ref), (c_hbm, c_ref))
        )
    ]
    for load in loads:
        load.start()
    for k in (EARLY, *(k for k in range(chunks) if k != EARLY)):
        x_load(k).start()

    @pl.when(core == 0)
    def _():
        sum_in[...] = jnp.zeros_like(sum_in)
        decay_in[...] = jnp.ones_like(decay_in)

    def decay_copy():
        return pltpu.make_async_remote_copy(
            src_ref=rows_e.at[2 * blocks + 1],
            dst_ref=decay_in,
            send_sem=decay_sem.at[0],
            recv_sem=decay_sem.at[1],
            device_id=sibling,
            device_id_type=MESH,
        )

    def sum_copy(k):
        return pltpu.make_async_remote_copy(
            src_ref=summary.at[:, chunk_of(k)],
            dst_ref=sum_in.at[:, chunk_of(k)],
            send_sem=sum_send.at[k],
            recv_sem=sum_recv.at[k],
            device_id=sibling,
            device_id_type=MESH,
        )

    def pass_copy(k):
        return pltpu.make_async_remote_copy(
            src_ref=begin.at[chunk_of(k)],
            dst_ref=begin.at[chunk_of(k)],
            send_sem=pass_send.at[k],
            recv_sem=pass_recv.at[k],
            device_id=sibling,
            device_id_type=MESH,
        )

    def spread_out(k):
        server, half = lax.rem(k, 2), k // 2

        def refs(dz, dx):
            q = dz + 1 + core
            to_x = lax.rem(x + dx, ROW)
            rows = pl.ds(pl.multiple_of(k * CHUNK + (q * ROW + to_x) * piece, piece), piece)
            who = (lax.rem(z + dz + rings, rings) * ROW + to_x, server, y)
            return snap_ref.at[:, rows], spread.at[half, q * ROW + x, pl.ds(2 * core, 2)], who

        def send(src, dst, who):
            pltpu.make_async_remote_copy(
                src_ref=src,
                dst_ref=dst,
                send_sem=spread_send.at[k],
                recv_sem=spread_recv.at[half],
                device_id=who,
                device_id_type=MESH,
            ).start()

        src, dst, who = refs(0, 0)

        @pl.when(core == server)
        def _():
            pltpu.make_async_copy(src, dst, spread_recv.at[half]).start()

        @pl.when(core != server)
        def _():
            send(src, dst, who)

        def one(i):
            dz = (lax.rem(i // ROW + 1, SPAN) - 1) * (1 - 2 * core)
            send(*refs(dz, lax.rem(i, ROW)))

        last = SPAN * ROW - 1
        loop(0, last, 5, lambda i: one(lax.rem(i + 7, last) + 1))

    def slot_of(r):
        return slot_ref[jnp.maximum(first_ref[r] + prefix_ref[r] - 1, 0)]

    def locate(r):
        slot = slot_of(r)
        low = lax.rem(slot, 4)
        q = lax.rem(z - slot // (4 * ROW) + 1 + low // 2 + rings, SPAN)
        place[r] = (q * ROW + lax.rem(slot // 4, ROW)) * 4 + low

    def pick(k):
        server, half = lax.rem(k, 2), k // 2
        here = spread.at[half]
        pltpu.make_async_copy(here, here, spread_recv.at[half]).wait()
        held[...] = here[...].reshape(held.shape)

        def choose(i):
            picked[half, i] = held[place[lax.rem(dp + i, plane)]]

        loop(0, plane, 8, choose)

        def refs(i):
            return picked.at[half, i], offered.at[k, z, x], (lax.rem(dp + i, plane), 0, y)

        def send(src, dst, who):
            pltpu.make_async_remote_copy(
                src_ref=src,
                dst_ref=dst,
                send_sem=pick_send.at[half],
                recv_sem=pick_recv.at[k],
                device_id=who,
                device_id_type=MESH,
            ).start()

        far = plane // 2 - 3
        loop(0, plane - 1, 10, lambda i: send(*refs(lax.rem(i + far, plane - 1) + 1)))
        src, dst, who = refs(0)

        @pl.when(server == 0)
        def _():
            pltpu.make_async_copy(src, dst, pick_recv.at[k]).start()

        @pl.when(server == 1)
        def _():
            send(src, dst, who)

    def gather(k):
        here = offered.at[k]
        pltpu.make_async_copy(here, here, pick_recv.at[k]).wait()
        came[...] = here[...]
        slot = slot_of(dp)
        low = lax.rem(slot, 4)
        for q in range(SPAN):
            at_z = lax.rem(slot // (4 * ROW) + q - 1 - low // 2 + rings, rings)
            rows = pl.ds(pl.multiple_of(k * CHUNK + q * ROW * piece, ROW * piece), ROW * piece)
            begin[rows, :] = came[at_z].reshape(ROW * piece, STATE)

    def y_copy(k, step):
        cols = chunk_of(k)
        there = pl.ds(pl.multiple_of(y * width + k * CHUNK, CHUNK), CHUNK)
        rows = pl.ds(pl.multiple_of(lax.rem(y + step, ranks) * quarter, quarter), quarter)
        if step == 0:
            return pltpu.make_async_copy(staged.at[rows, cols], o_ref.at[:, there], own_sem.at[k])
        return pltpu.make_async_remote_copy(
            src_ref=staged.at[rows, cols],
            dst_ref=o_ref.at[:, there],
            send_sem=y_send.at[k, step - 1],
            recv_sem=y_recv.at[k, step - 1],
            device_id=peer(step),
            device_id_type=MESH,
        )

    def map_copies(step):
        rows = pl.ds(pl.multiple_of(lax.rem(y + step, ranks) * quarter, quarter), quarter)
        pairs = ((c_ref.at[rows], c_in), (reached.at[pl.ds(EARLY * 8, 8), rows], decays_in))
        return [
            pltpu.make_async_remote_copy(
                src_ref=src,
                dst_ref=dst.at[step - 1],
                send_sem=map_send.at[step - 1, i],
                recv_sem=map_recv.at[step - 1, i],
                device_id=peer(step),
                device_id_type=MESH,
            )
            for i, (src, dst) in enumerate(pairs)
        ]

    def early_copy(k, step):
        rows = pl.ds(pl.multiple_of(lax.rem(y + step, ranks) * quarter, quarter), quarter)
        return pltpu.make_async_remote_copy(
            src_ref=staged.at[rows, chunk_of(k)],
            dst_ref=early.at[step - 1],
            send_sem=early_send.at[step - 1],
            recv_sem=early_recv.at[step - 1],
            device_id=peer(step),
            device_id_type=MESH,
        )

    def state_copy(k, step):
        return pltpu.make_async_remote_copy(
            src_ref=entering.at[:, chunk_of(k)],
            dst_ref=state_in.at[step - 1],
            send_sem=state_send.at[step - 1],
            recv_sem=state_recv.at[step - 1],
            device_id=peer(step),
            device_id_type=MESH,
        )

    def late_copy(k, step):
        whose = lax.rem(y + ranks - step, ranks)
        there = pl.ds(pl.multiple_of(whose * width + k * CHUNK, CHUNK), CHUNK)
        return pltpu.make_async_copy(
            early.at[step - 1], o_ref.at[:, there], late_sem.at[step - 1]
        )

    def send_early(k):
        cols = chunk_of(k)
        for step in (2, 1, 3):
            rows = pl.ds(pl.multiple_of(lax.rem(y + step, ranks) * quarter, quarter), quarter)
            staged[rows, cols] = acc[rows, cols].astype(BF16)
            early_copy(k, step).start()

    def finish_late(k):
        spot = lax.broadcasted_iota(jnp.int32, (BLOCK, CHUNK), 0)
        head = lax.broadcasted_iota(jnp.int32, (BLOCK, CHUNK), 1) // HEAD_DIM
        widen = (spot == head).astype(F32)
        for step in (1, 3, 2):
            early_copy(k, step).wait_recv()
            state_copy(k, step).wait_recv()
            entered = state_in[step - 1]
            for half in range(quarter // BLOCK):
                at = pl.ds(half * BLOCK, BLOCK)
                decays = decays_in[step - 1, :, at]
                padded = jnp.concatenate(
                    [decays, jnp.zeros((BLOCK - decays.shape[0], BLOCK), F32)], axis=0
                )
                grown = jnp.dot(
                    padded.T,
                    widen,
                    precision=lax.Precision.HIGHEST,
                    preferred_element_type=F32,
                )
                mixed = jnp.dot(c_in[step - 1, at, :], entered, preferred_element_type=F32)
                early[step - 1, at, :] = (
                    early[step - 1, at, :].astype(F32) + grown * mixed
                ).astype(BF16)
            late_copy(k, step).start()

    def finish(k):
        @pl.when(core == 0)
        def _():
            gather(k)
            pass_copy(k).start()

        @pl.when(core == 1)
        def _():
            sum_copy(k).wait_recv()
            pass_copy(k).wait_recv()

        cols = chunk_of(k)
        for i in range(CHUNK // STATE):
            part = pl.ds(pl.multiple_of(k * CHUNK + i * STATE, STATE), STATE)
            loaded = begin[part, :].astype(F32).T
            entering[:, part] = (
                decay_in[0:1, part] * loaded + sum_in[:, part].astype(F32)
            ).astype(BF16)
        entered = entering[:, cols]

        def output(step):
            rows = pl.ds(pl.multiple_of(lax.rem(y + step, ranks) * quarter, quarter), quarter)
            mixed = jnp.dot(c_ref[rows, :], entered, preferred_element_type=F32)
            staged[rows, cols] = (acc[rows, cols] + growth[rows, cols] * mixed).astype(BF16)
            y_copy(k, step).start()

        @pl.when(k == EARLY)
        def _():
            for step in (2, 1, 3):
                state_copy(k, step).start()

        @pl.when(k != EARLY)
        def _():
            for step in (2, 1, 3):
                output(step)

        output(0)

    released_late = z >= rings // 4

    def enter():
        pl.semaphore_wait(barrier, 2 * plane - 1 + ranks - 1)
        spread_out(0)

        @pl.when(core == 0)
        def _():
            decay_copy().start()

    def stage(s, _):
        scanned = jnp.where(s < 2, 1 - s, s)

        @pl.when(s < chunks)
        def _():
            x_load(scanned).wait()
            local_chunk(
                blocks,
                scanned,
                x_ref,
                c_ref,
                sm,
                bt,
                run_t,
                urow,
                fac,
                rows_e,
                state,
                summary,
                acc,
                growth,
            )

        @pl.when(s == 0)
        def _():
            pl.when(jnp.logical_not(released_late))(enter)
            send_early(EARLY)
            for step in (2, 1, 3):
                for copy in map_copies(step):
                    copy.start()

        @pl.when(s < chunks)
        def _():
            @pl.when(core == 0)
            def _():
                sum_copy(scanned).start()

            served = jnp.logical_and(s == 0, released_late)

            @pl.when(jnp.logical_and(core == 0, jnp.logical_and(lax.rem(s, 2) == 0, jnp.logical_not(served))))
            def _():
                pick(s)

        @pl.when(s == 0)
        def _():
            spread_out(1)

            @pl.when(core == 1)
            def _():
                decay_copy().wait_recv()

        @pl.when(s < chunks - 2)
        def _():
            spread_out(s + 2)

        @pl.when(s >= 1)
        def _():
            finish(s - 1)

        @pl.when(jnp.logical_and(core == 1, jnp.logical_and(s < chunks, lax.rem(s, 2) == 1)))
        def _():
            pick(s)

        return 0

    for load in loads:
        load.wait()
    prepare(
        blocks, b_ref, c_ref, ld_ref, dt_ref, gain_ref, sm, bt, run_t, urow, fac, rows_e, reached
    )
    pl.when(released_late)(enter)
    loop(0, plane, 4, locate)

    @pl.when(jnp.logical_and(core == 0, released_late))
    def _():
        pick(0)

    lax.fori_loop(0, chunks + 1, stage, 0)
    for step in (1, 3, 2):
        for copy in map_copies(step):
            copy.wait()

    finish_late(EARLY)

    @pl.when(core == 0)
    def _():
        decay_copy().wait_send()

    def drain(k, _):
        y_copy(k, 0).wait()

        @pl.when(k == EARLY)
        def _():
            for step in range(1, ranks):
                early_copy(k, step).wait_send()
                state_copy(k, step).wait_send()
                late_copy(k, step).wait()

        @pl.when(k != EARLY)
        def _():
            for step in range(1, ranks):
                y_copy(k, step).wait()

        server, half = lax.rem(k, 2), k // 2
        pieces = picked.at[half]

        @pl.when(core == server)
        def _():
            sent = pieces.at[pl.ds(0, plane - 2)]
            pltpu.make_async_copy(sent, sent, spread_send.at[k]).wait()

        @pl.when(core != server)
        def _():
            pltpu.make_async_copy(pieces, pieces, spread_send.at[k]).wait()

        @pl.when(jnp.logical_and(core == 0, server == 0))
        def _():
            sent = pieces.at[pl.ds(0, plane - 1)]
            pltpu.make_async_copy(sent, sent, pick_send.at[half]).wait()

        @pl.when(jnp.logical_and(core == 1, server == 1))
        def _():
            pltpu.make_async_copy(pieces, pieces, pick_send.at[half]).wait()

        @pl.when(core == 0)
        def _():
            sum_copy(k).wait_send()
            pass_copy(k).wait_send()

        return 0

    lax.fori_loop(0, chunks, drain, 0)


def copy_kernel(parts, in_ref, out_ref, held, in_sem, out_sem):
    rows = in_ref.shape[0] // parts

    def part(i):
        return pl.ds(i * rows, rows)

    reads = [
        pltpu.make_async_copy(in_ref.at[part(i)], held.at[part(i)], in_sem.at[i])
        for i in range(parts)
    ]
    writes = [
        pltpu.make_async_copy(held.at[part(i)], out_ref.at[part(i)], out_sem.at[i])
        for i in range(parts)
    ]
    for read in reads:
        read.start()
    for read, write in zip(reads, writes):
        read.wait()
        write.start()
    for write in writes:
        write.wait()


def per_device(
    tokens,
    input_map,
    output_map,
    log_decay,
    step_size,
    skip_gain,
    snapshots,
    first_snap,
    prefix_kilo,
    snap_slot,
):
    length, width = tokens.shape[1:]
    heads = log_decay.shape[1]
    blocks = length // BLOCK
    ranks = lax.axis_size("tensor")
    chunks = width // CHUNK
    out_shape = (length // ranks, width * ranks)
    plane = lax.axis_size("dp")
    piece = CHUNK // (SPAN * ROW)
    hbm, smem = pl.BlockSpec(memory_space=pl.ANY), pl.BlockSpec(memory_space=pltpu.SMEM)
    dma = pltpu.SemaphoreType.DMA
    mixed = pl.pallas_call(
        functools.partial(kernel, blocks, ranks),
        out_shape=jax.ShapeDtypeStruct(out_shape, BF16),
        in_specs=[smem] * 3 + [hbm] * 5 + [pl.BlockSpec(memory_space=pltpu.VMEM), hbm],
        out_specs=hbm,
        scratch_shapes=[
            pltpu.VMEM((length, width), BF16),
            pltpu.VMEM((length, STATE), BF16),
            pltpu.VMEM((length, STATE), BF16),
            pltpu.VMEM((heads, length), F32),
            pltpu.VMEM((heads, length), F32),
            pltpu.VMEM((length, BLOCK), F32),
            pltpu.VMEM((length, BLOCK), F32),
            pltpu.VMEM((length, BLOCK), F32),
            pltpu.VMEM((heads, length), F32),
            pltpu.VMEM((heads, length), F32),
            pltpu.VMEM((2 * blocks + 2, 8, width), F32),
            pltpu.VMEM((STATE, CHUNK), F32),
            pltpu.VMEM((STATE, width), BF16),
            pltpu.VMEM((length, width), F32),
            pltpu.VMEM((length, width), F32),
            pltpu.VMEM((length, width), BF16),
            pltpu.VMEM((STATE, width), BF16),
            pltpu.VMEM((8, width), F32),
            pltpu.VMEM((width, STATE), BF16),
            pltpu.VMEM((chunks // 2, SPAN * ROW, 4, piece, STATE), BF16),
            pltpu.VMEM((SPAN * ROW * 4, piece, STATE), BF16),
            pltpu.VMEM((chunks // 2, plane, piece, STATE), BF16),
            pltpu.VMEM((chunks, plane // ROW, ROW, piece, STATE), BF16),
            pltpu.VMEM((plane // ROW, ROW, piece, STATE), BF16),
            pltpu.SMEM((plane,), jnp.int32),
            pltpu.VMEM((heads, length), F32),
            pltpu.VMEM((STATE, width), BF16),
            pltpu.VMEM((ranks - 1, length // ranks, CHUNK), BF16),
            pltpu.VMEM((ranks - 1, length // ranks, STATE), BF16),
            pltpu.VMEM((ranks - 1, 8, length // ranks), F32),
            pltpu.VMEM((ranks - 1, STATE, CHUNK), BF16),
            dma((4,)),
            dma((chunks,)),
            dma((chunks,)),
            dma((chunks // 2,)),
            dma((chunks // 2,)),
            dma((chunks,)),
            dma((2,)),
            dma((chunks,)),
            dma((chunks,)),
            dma((chunks,)),
            dma((chunks,)),
            dma((chunks, ranks - 1)),
            dma((chunks, ranks - 1)),
            dma((chunks,)),
            dma((ranks - 1, 2)),
            dma((ranks - 1, 2)),
            dma((ranks - 1,)),
            dma((ranks - 1,)),
            dma((ranks - 1,)),
            dma((ranks - 1,)),
            dma((ranks - 1,)),
        ],
        compiler_params=pltpu.CompilerParams(
            collective_id=0, has_side_effects=True, vmem_limit_bytes=56 * 2**20
        ),
        name="scan_and_send",
    )(
        first_snap,
        prefix_kilo,
        snap_slot,
        tokens[0],
        input_map[0],
        output_map[0],
        log_decay[0],
        step_size[0],
        skip_gain.reshape(1, heads),
        snapshots.reshape(snapshots.shape[0], width, STATE),
    )
    parts = 4
    result = pl.pallas_call(
        functools.partial(copy_kernel, parts),
        out_shape=jax.ShapeDtypeStruct(out_shape, BF16),
        in_specs=[pl.BlockSpec(memory_space=pl.ANY)],
        out_specs=pl.BlockSpec(memory_space=pl.ANY),
        scratch_shapes=[
            pltpu.VMEM(out_shape, BF16),
            pltpu.SemaphoreType.DMA((parts,)),
            pltpu.SemaphoreType.DMA((parts,)),
        ],
        compiler_params=pltpu.CompilerParams(vmem_limit_bytes=60 * 2**20),
        name="place_result",
    )(mixed)
    return result[None]


def solution(mesh):
    placed = (
        P("dp", "seq", "tensor"),
        P("dp", "seq", "tensor"),
        P("dp", "seq", "tensor"),
        P("dp", "tensor", "seq"),
        P("dp", "tensor", "seq"),
        P("tensor"),
        P(("dp", "seq"), "tensor", None, None),
        P(),
        P(),
        P(),
    )
    return jax.shard_map(
        per_device,
        mesh=mesh,
        in_specs=placed,
        out_specs=P("dp", ("seq", "tensor"), None),
        check_vma=False,
    )
```

```python
import functools

import jax
import jax.numpy as jnp
from jax import lax
from jax.experimental import pallas as pl
from jax.experimental.pallas import tpu as pltpu
from jax.sharding import PartitionSpec as P

HEAD_DIM = 64
STATE = 128
BLOCK = 128
CHUNK = 8 * HEAD_DIM
LOG2E = 1.4426950408889634
ROW = 4
SPAN = 4
EARLY = 1
MESH = pl.DeviceIdType.MESH
F32 = jnp.float32
BF16 = jnp.bfloat16


def prepare(
    blocks, b_ref, c_ref, ld_ref, dt_ref, gain_ref, sm, bt, run_t, urow, fac, rows_e, reached
):
    heads = ld_ref.shape[0]
    width = heads * HEAD_DIM
    row = lax.broadcasted_iota(jnp.int32, (BLOCK, BLOCK), 0)
    col = lax.broadcasted_iota(jnp.int32, (BLOCK, BLOCK), 1)
    upto = (row <= col).astype(F32)
    ends = []
    so_far = jnp.zeros((heads, 1), F32)
    for b in range(blocks):
        at = pl.ds(b * BLOCK, BLOCK)
        run = jnp.dot(
            ld_ref[:, at], upto, precision=lax.Precision.HIGHEST, preferred_element_type=F32
        )
        run = run * LOG2E
        step = dt_ref[:, at]
        end = run[:, BLOCK - 1 :]
        urow[:, at] = run - jnp.log2(step)
        fac[:, at] = jnp.exp2(end - run) * step
        reached[:, at] = jnp.exp2(run + so_far)
        so_far = so_far + end
        padded = jnp.concatenate([run, jnp.zeros((BLOCK - heads, BLOCK), F32)], axis=0)
        turned = padded.T
        run_t[at, :] = turned
        ends.append(turned[BLOCK - 1 :, :])
        inputs = b_ref[at, :]
        scores = lax.dot_general(
            c_ref[at, :], inputs, (((1,), (1,)), ((), ())), preferred_element_type=F32
        )
        sm[at, :] = jnp.where(row >= col, scores, 0.0)
        bt[at, :] = inputs.astype(F32).T
    stacked = jnp.concatenate(ends, axis=0)
    pad = (-stacked.shape[0]) % 8
    if pad:
        stacked = jnp.concatenate([stacked, jnp.zeros((pad, BLOCK), F32)], axis=0)
    spot = lax.broadcasted_iota(jnp.int32, (BLOCK, width), 0)
    head = lax.broadcasted_iota(jnp.int32, (BLOCK, width), 1) // HEAD_DIM
    spread = (spot == head).astype(F32)
    wide = jnp.dot(stacked, spread, precision=lax.Precision.HIGHEST, preferred_element_type=F32)
    gain = jnp.dot(
        gain_ref[...], spread[:heads], precision=lax.Precision.HIGHEST, preferred_element_type=F32
    )
    reach = jnp.zeros((1, width), F32)
    for b in range(blocks):
        end = wide[b : b + 1, :]
        rows_e[b] = jnp.broadcast_to(jnp.exp2(end), (8, width))
        rows_e[blocks + 1 + b] = jnp.broadcast_to(jnp.exp2(reach), (8, width))
        reach = reach + end
    rows_e[blocks] = jnp.broadcast_to(gain, (8, width))
    rows_e[2 * blocks + 1] = jnp.broadcast_to(jnp.exp2(reach), (8, width))


def local_chunk(
    blocks, k, x_ref, c_ref, sm, bt, run_t, urow, fac, rows_e, state, summary, acc, growth
):
    cols = pl.ds(pl.multiple_of(k * CHUNK, CHUNK), CHUNK)
    octet = pl.ds(pl.multiple_of(k * 8, 8), 8)
    pair_width = 2 * HEAD_DIM
    first = lax.broadcasted_iota(jnp.int32, (1, pair_width), 1) < HEAD_DIM
    keep0 = jnp.where(first, 1.0, 0.0).astype(BF16)
    keep1 = jnp.where(first, 0.0, 1.0).astype(BF16)
    state[...] = jnp.zeros_like(state)

    def one(b, _):
        at = pl.ds(pl.multiple_of(b * BLOCK, BLOCK), BLOCK)
        turned = pltpu.roll(run_t[at, :], lax.rem(BLOCK - 8 * k, BLOCK), 1)
        u = urow[octet, at]
        f = fac[octet, at]
        carried = jnp.dot(c_ref[at, :], state[...].astype(BF16), preferred_element_type=F32)
        for j in range(CHUNK // pair_width):
            mine = slice(j * pair_width, (j + 1) * pair_width)
            here = pl.ds(pl.multiple_of(k * CHUNK + j * pair_width, pair_width), pair_width)
            h0, h1 = slice(2 * j, 2 * j + 1), slice(2 * j + 1, 2 * j + 2)
            scores = sm[at, :]
            back = bt[at, :]
            run0 = jnp.broadcast_to(turned[:, h0], (BLOCK, BLOCK))
            run1 = jnp.broadcast_to(turned[:, h1], (BLOCK, BLOCK))
            w0 = (scores * jnp.exp2(jnp.minimum(run0 - u[h0], 64.0))).astype(BF16)
            w1 = (scores * jnp.exp2(jnp.minimum(run1 - u[h1], 64.0))).astype(BF16)
            b0 = (back * f[h0]).astype(BF16)
            b1 = (back * f[h1]).astype(BF16)
            x = x_ref[at, here]
            left = jnp.concatenate(
                [jnp.concatenate([w0, w1], axis=1), jnp.concatenate([b0, b1], axis=1)], axis=0
            )
            right = jnp.concatenate([x * keep0, x * keep1], axis=0)
            both = jnp.dot(left, right, preferred_element_type=F32)
            grown = jnp.exp2(jnp.where(first, run0, run1))
            acc[at, here] = (
                both[:BLOCK]
                + grown * carried[:, mine]
                + x.astype(F32) * rows_e[blocks, :, here][0:1, :]
            )
            growth[at, here] = grown * rows_e[blocks + 1 + b, :, here][0:1, :]
            state[:, mine] = rows_e[b, :, here][0:1, :] * state[:, mine] + both[BLOCK:]
        return 0

    lax.fori_loop(0, blocks, one, 0, unroll=4)
    summary[:, cols] = state[...].astype(BF16)


def loop(start, stop, group, body):
    def step(j, _):
        for i in range(group):
            body(start + j * group + i)
        return 0

    steps = (stop - start) // group
    lax.fori_loop(0, steps, step, 0)
    for i in range(start + steps * group, stop):
        body(i)


def kernel(
    blocks,
    ranks,
    first_ref,
    prefix_ref,
    slot_ref,
    x_hbm,
    b_hbm,
    c_hbm,
    ld_hbm,
    dt_hbm,
    gain_ref,
    snap_ref,
    o_ref,
    x_ref,
    b_ref,
    c_ref,
    ld_ref,
    dt_ref,
    sm,
    bt,
    run_t,
    urow,
    fac,
    rows_e,
    state,
    summary,
    acc,
    growth,
    staged,
    sum_in,
    decay_in,
    begin,
    spread,
    held,
    picked,
    offered,
    came,
    place,
    reached,
    entering,
    early,
    c_in,
    decays_in,
    state_in,
    load_sem,
    x_sem,
    spread_send,
    spread_recv,
    pick_send,
    pick_recv,
    decay_sem,
    sum_send,
    sum_recv,
    pass_send,
    pass_recv,
    y_send,
    y_recv,
    own_sem,
    map_send,
    map_recv,
    early_send,
    early_recv,
    state_send,
    state_recv,
    late_sem,
):
    dp, core, y = lax.axis_index("dp"), lax.axis_index("seq"), lax.axis_index("tensor")
    z, x = dp // ROW, dp % ROW
    plane = lax.axis_size("dp")
    rings = plane // ROW
    sibling = (dp, 1 - core, y)
    quarter = blocks * BLOCK // ranks
    width = x_ref.shape[1]
    chunks = width // CHUNK
    piece = CHUNK // (SPAN * ROW)

    def peer(step):
        return (dp, core, lax.rem(y + step, ranks))

    def chunk_of(k):
        return pl.ds(pl.multiple_of(k * CHUNK, CHUNK), CHUNK)

    def x_load(k):
        cols = chunk_of(k)
        return pltpu.make_async_copy(x_hbm.at[:, cols], x_ref.at[:, cols], x_sem.at[k])

    barrier = pltpu.get_barrier_semaphore()

    def greet(i):
        who = (lax.rem(dp + i // 2, plane), lax.rem(core + i, 2), y)
        pl.semaphore_signal(barrier, inc=1, device_id=who, device_id_type=MESH)

    loop(1, 2 * plane, 9, greet)
    for step in range(1, ranks):
        pl.semaphore_signal(barrier, inc=1, device_id=peer(step), device_id_type=MESH)

    loads = [
        pltpu.make_async_copy(src, dst, load_sem.at[i])
        for i, (src, dst) in enumerate(
            ((ld_hbm, ld_ref), (dt_hbm, dt_ref), (b_hbm, b_ref), (c_hbm, c_ref))
        )
    ]
    for load in loads:
        load.start()
    for k in (EARLY, *(k for k in range(chunks) if k != EARLY)):
        x_load(k).start()

    @pl.when(core == 0)
    def _():
        sum_in[...] = jnp.zeros_like(sum_in)
        decay_in[...] = jnp.ones_like(decay_in)

    def decay_copy():
        return pltpu.make_async_remote_copy(
            src_ref=rows_e.at[2 * blocks + 1],
            dst_ref=decay_in,
            send_sem=decay_sem.at[0],
            recv_sem=decay_sem.at[1],
            device_id=sibling,
            device_id_type=MESH,
        )

    def sum_copy(k):
        return pltpu.make_async_remote_copy(
            src_ref=summary.at[:, chunk_of(k)],
            dst_ref=sum_in.at[:, chunk_of(k)],
            send_sem=sum_send.at[k],
            recv_sem=sum_recv.at[k],
            device_id=sibling,
            device_id_type=MESH,
        )

    def pass_copy(k):
        return pltpu.make_async_remote_copy(
            src_ref=begin.at[chunk_of(k)],
            dst_ref=begin.at[chunk_of(k)],
            send_sem=pass_send.at[k],
            recv_sem=pass_recv.at[k],
            device_id=sibling,
            device_id_type=MESH,
        )

    def spread_out(k):
        server, half = lax.rem(k, 2), k // 2

        def refs(dz, dx):
            q = dz + 1 + core
            to_x = lax.rem(x + dx, ROW)
            rows = pl.ds(pl.multiple_of(k * CHUNK + (q * ROW + to_x) * piece, piece), piece)
            who = (lax.rem(z + dz + rings, rings) * ROW + to_x, server, y)
            return snap_ref.at[:, rows], spread.at[half, q * ROW + x, pl.ds(2 * core, 2)], who

        def send(src, dst, who):
            pltpu.make_async_remote_copy(
                src_ref=src,
                dst_ref=dst,
                send_sem=spread_send.at[k],
                recv_sem=spread_recv.at[half],
                device_id=who,
                device_id_type=MESH,
            ).start()

        src, dst, who = refs(0, 0)

        @pl.when(core == server)
        def _():
            pltpu.make_async_copy(src, dst, spread_recv.at[half]).start()

        @pl.when(core != server)
        def _():
            send(src, dst, who)

        def one(i):
            dz = (lax.rem(i // ROW + 1, SPAN) - 1) * (1 - 2 * core)
            send(*refs(dz, lax.rem(i, ROW)))

        last = SPAN * ROW - 1
        loop(0, last, 5, lambda i: one(lax.rem(i + 7, last) + 1))

    def slot_of(r):
        return slot_ref[jnp.maximum(first_ref[r] + prefix_ref[r] - 1, 0)]

    def locate(r):
        slot = slot_of(r)
        low = lax.rem(slot, 4)
        q = lax.rem(z - slot // (4 * ROW) + 1 + low // 2 + rings, SPAN)
        place[r] = (q * ROW + lax.rem(slot // 4, ROW)) * 4 + low

    def pick(k):
        server, half = lax.rem(k, 2), k // 2
        here = spread.at[half]
        pltpu.make_async_copy(here, here, spread_recv.at[half]).wait()
        held[...] = here[...].reshape(held.shape)

        def choose(i):
            picked[half, i] = held[place[lax.rem(dp + i, plane)]]

        loop(0, plane, 8, choose)

        def refs(i):
            return picked.at[half, i], offered.at[k, z, x], (lax.rem(dp + i, plane), 0, y)

        def send(src, dst, who):
            pltpu.make_async_remote_copy(
                src_ref=src,
                dst_ref=dst,
                send_sem=pick_send.at[half],
                recv_sem=pick_recv.at[k],
                device_id=who,
                device_id_type=MESH,
            ).start()

        far = plane // 2 - 3
        loop(0, plane - 1, 10, lambda i: send(*refs(lax.rem(i + far, plane - 1) + 1)))
        src, dst, who = refs(0)

        @pl.when(server == 0)
        def _():
            pltpu.make_async_copy(src, dst, pick_recv.at[k]).start()

        @pl.when(server == 1)
        def _():
            send(src, dst, who)

    def gather(k):
        here = offered.at[k]
        pltpu.make_async_copy(here, here, pick_recv.at[k]).wait()
        came[...] = here[...]
        slot = slot_of(dp)
        low = lax.rem(slot, 4)
        for q in range(SPAN):
            at_z = lax.rem(slot // (4 * ROW) + q - 1 - low // 2 + rings, rings)
            rows = pl.ds(pl.multiple_of(k * CHUNK + q * ROW * piece, ROW * piece), ROW * piece)
            begin[rows, :] = came[at_z].reshape(ROW * piece, STATE)

    def y_copy(k, step):
        cols = chunk_of(k)
        there = pl.ds(pl.multiple_of(y * width + k * CHUNK, CHUNK), CHUNK)
        rows = pl.ds(pl.multiple_of(lax.rem(y + step, ranks) * quarter, quarter), quarter)
        if step == 0:
            return pltpu.make_async_copy(staged.at[rows, cols], o_ref.at[:, there], own_sem.at[k])
        return pltpu.make_async_remote_copy(
            src_ref=staged.at[rows, cols],
            dst_ref=o_ref.at[:, there],
            send_sem=y_send.at[k, step - 1],
            recv_sem=y_recv.at[k, step - 1],
            device_id=peer(step),
            device_id_type=MESH,
        )

    def map_copies(step):
        rows = pl.ds(pl.multiple_of(lax.rem(y + step, ranks) * quarter, quarter), quarter)
        pairs = ((c_ref.at[rows], c_in), (reached.at[pl.ds(EARLY * 8, 8), rows], decays_in))
        return [
            pltpu.make_async_remote_copy(
                src_ref=src,
                dst_ref=dst.at[step - 1],
                send_sem=map_send.at[step - 1, i],
                recv_sem=map_recv.at[step - 1, i],
                device_id=peer(step),
                device_id_type=MESH,
            )
            for i, (src, dst) in enumerate(pairs)
        ]

    def early_copy(k, step):
        rows = pl.ds(pl.multiple_of(lax.rem(y + step, ranks) * quarter, quarter), quarter)
        return pltpu.make_async_remote_copy(
            src_ref=staged.at[rows, chunk_of(k)],
            dst_ref=early.at[step - 1],
            send_sem=early_send.at[step - 1],
            recv_sem=early_recv.at[step - 1],
            device_id=peer(step),
            device_id_type=MESH,
        )

    def state_copy(k, step):
        return pltpu.make_async_remote_copy(
            src_ref=entering.at[:, chunk_of(k)],
            dst_ref=state_in.at[step - 1],
            send_sem=state_send.at[step - 1],
            recv_sem=state_recv.at[step - 1],
            device_id=peer(step),
            device_id_type=MESH,
        )

    def late_copy(k, step):
        whose = lax.rem(y + ranks - step, ranks)
        there = pl.ds(pl.multiple_of(whose * width + k * CHUNK, CHUNK), CHUNK)
        return pltpu.make_async_copy(
            early.at[step - 1], o_ref.at[:, there], late_sem.at[step - 1]
        )

    def send_early(k):
        cols = chunk_of(k)
        for step in (2, 1, 3):
            rows = pl.ds(pl.multiple_of(lax.rem(y + step, ranks) * quarter, quarter), quarter)
            staged[rows, cols] = acc[rows, cols].astype(BF16)
            early_copy(k, step).start()

    def finish_late(k):
        spot = lax.broadcasted_iota(jnp.int32, (BLOCK, CHUNK), 0)
        head = lax.broadcasted_iota(jnp.int32, (BLOCK, CHUNK), 1) // HEAD_DIM
        widen = (spot == head).astype(F32)
        for step in (1, 3, 2):
            early_copy(k, step).wait_recv()
            state_copy(k, step).wait_recv()
            entered = state_in[step - 1]
            for half in range(quarter // BLOCK):
                at = pl.ds(half * BLOCK, BLOCK)
                decays = decays_in[step - 1, :, at]
                padded = jnp.concatenate(
                    [decays, jnp.zeros((BLOCK - decays.shape[0], BLOCK), F32)], axis=0
                )
                grown = jnp.dot(
                    padded.T,
                    widen,
                    precision=lax.Precision.HIGHEST,
                    preferred_element_type=F32,
                )
                mixed = jnp.dot(c_in[step - 1, at, :], entered, preferred_element_type=F32)
                early[step - 1, at, :] = (
                    early[step - 1, at, :].astype(F32) + grown * mixed
                ).astype(BF16)
            late_copy(k, step).start()

    def finish(k):
        @pl.when(core == 0)
        def _():
            gather(k)
            pass_copy(k).start()

        @pl.when(core == 1)
        def _():
            sum_copy(k).wait_recv()
            pass_copy(k).wait_recv()

        cols = chunk_of(k)
        for i in range(CHUNK // STATE):
            part = pl.ds(pl.multiple_of(k * CHUNK + i * STATE, STATE), STATE)
            loaded = begin[part, :].astype(F32).T
            entering[:, part] = (
                decay_in[0:1, part] * loaded + sum_in[:, part].astype(F32)
            ).astype(BF16)
        entered = entering[:, cols]

        def output(step):
            rows = pl.ds(pl.multiple_of(lax.rem(y + step, ranks) * quarter, quarter), quarter)
            mixed = jnp.dot(c_ref[rows, :], entered, preferred_element_type=F32)
            staged[rows, cols] = (acc[rows, cols] + growth[rows, cols] * mixed).astype(BF16)
            y_copy(k, step).start()

        @pl.when(k == EARLY)
        def _():
            for step in (2, 1, 3):
                state_copy(k, step).start()

        @pl.when(k != EARLY)
        def _():
            for step in (2, 1, 3):
                output(step)

        output(0)

    released_late = z >= rings // 4

    def enter():
        pl.semaphore_wait(barrier, 2 * plane - 1 + ranks - 1)
        spread_out(0)

        @pl.when(core == 0)
        def _():
            decay_copy().start()

    def stage(s, _):
        scanned = jnp.where(s < 2, 1 - s, s)

        @pl.when(s < chunks)
        def _():
            x_load(scanned).wait()
            local_chunk(
                blocks,
                scanned,
                x_ref,
                c_ref,
                sm,
                bt,
                run_t,
                urow,
                fac,
                rows_e,
                state,
                summary,
                acc,
                growth,
            )

        @pl.when(s == 0)
        def _():
            pl.when(jnp.logical_not(released_late))(enter)
            send_early(EARLY)
            for step in (2, 1, 3):
                for copy in map_copies(step):
                    copy.start()

        @pl.when(s < chunks)
        def _():
            @pl.when(core == 0)
            def _():
                sum_copy(scanned).start()

            served = jnp.logical_and(s == 0, released_late)

            @pl.when(jnp.logical_and(core == 0, jnp.logical_and(lax.rem(s, 2) == 0, jnp.logical_not(served))))
            def _():
                pick(s)

        @pl.when(s == 0)
        def _():
            spread_out(1)

            @pl.when(core == 1)
            def _():
                decay_copy().wait_recv()

        @pl.when(s < chunks - 2)
        def _():
            spread_out(s + 2)

        @pl.when(s >= 1)
        def _():
            finish(s - 1)

        @pl.when(jnp.logical_and(core == 1, jnp.logical_and(s < chunks, lax.rem(s, 2) == 1)))
        def _():
            pick(s)

        return 0

    for load in loads:
        load.wait()
    prepare(
        blocks, b_ref, c_ref, ld_ref, dt_ref, gain_ref, sm, bt, run_t, urow, fac, rows_e, reached
    )
    pl.when(released_late)(enter)
    loop(0, plane, 4, locate)

    @pl.when(jnp.logical_and(core == 0, released_late))
    def _():
        pick(0)

    lax.fori_loop(0, chunks + 1, stage, 0)
    for step in (1, 3, 2):
        for copy in map_copies(step):
            copy.wait()

    finish_late(EARLY)

    @pl.when(core == 0)
    def _():
        decay_copy().wait_send()

    def drain(k, _):
        y_copy(k, 0).wait()

        @pl.when(k == EARLY)
        def _():
            for step in range(1, ranks):
                early_copy(k, step).wait_send()
                state_copy(k, step).wait_send()
                late_copy(k, step).wait()

        @pl.when(k != EARLY)
        def _():
            for step in range(1, ranks):
                y_copy(k, step).wait()

        server, half = lax.rem(k, 2), k // 2
        pieces = picked.at[half]

        @pl.when(core == server)
        def _():
            sent = pieces.at[pl.ds(0, plane - 2)]
            pltpu.make_async_copy(sent, sent, spread_send.at[k]).wait()

        @pl.when(core != server)
        def _():
            pltpu.make_async_copy(pieces, pieces, spread_send.at[k]).wait()

        @pl.when(jnp.logical_and(core == 0, server == 0))
        def _():
            sent = pieces.at[pl.ds(0, plane - 1)]
            pltpu.make_async_copy(sent, sent, pick_send.at[half]).wait()

        @pl.when(jnp.logical_and(core == 1, server == 1))
        def _():
            pltpu.make_async_copy(pieces, pieces, pick_send.at[half]).wait()

        @pl.when(core == 0)
        def _():
            sum_copy(k).wait_send()
            pass_copy(k).wait_send()

        return 0

    lax.fori_loop(0, chunks, drain, 0)


def copy_kernel(parts, in_ref, out_ref, held, in_sem, out_sem):
    rows = in_ref.shape[0] // parts

    def part(i):
        return pl.ds(i * rows, rows)

    reads = [
        pltpu.make_async_copy(in_ref.at[part(i)], held.at[part(i)], in_sem.at[i])
        for i in range(parts)
    ]
    writes = [
        pltpu.make_async_copy(held.at[part(i)], out_ref.at[part(i)], out_sem.at[i])
        for i in range(parts)
    ]
    for read in reads:
        read.start()
    for read, write in zip(reads, writes):
        read.wait()
        write.start()
    for write in writes:
        write.wait()


def per_device(
    tokens,
    input_map,
    output_map,
    log_decay,
    step_size,
    skip_gain,
    snapshots,
    first_snap,
    prefix_kilo,
    snap_slot,
):
    length, width = tokens.shape[1:]
    heads = log_decay.shape[1]
    blocks = length // BLOCK
    ranks = lax.axis_size("tensor")
    chunks = width // CHUNK
    out_shape = (length // ranks, width * ranks)
    plane = lax.axis_size("dp")
    piece = CHUNK // (SPAN * ROW)
    hbm, smem = pl.BlockSpec(memory_space=pl.ANY), pl.BlockSpec(memory_space=pltpu.SMEM)
    dma = pltpu.SemaphoreType.DMA
    mixed = pl.pallas_call(
        functools.partial(kernel, blocks, ranks),
        out_shape=jax.ShapeDtypeStruct(out_shape, BF16),
        in_specs=[smem] * 3 + [hbm] * 5 + [pl.BlockSpec(memory_space=pltpu.VMEM), hbm],
        out_specs=hbm,
        scratch_shapes=[
            pltpu.VMEM((length, width), BF16),
            pltpu.VMEM((length, STATE), BF16),
            pltpu.VMEM((length, STATE), BF16),
            pltpu.VMEM((heads, length), F32),
            pltpu.VMEM((heads, length), F32),
            pltpu.VMEM((length, BLOCK), F32),
            pltpu.VMEM((length, BLOCK), F32),
            pltpu.VMEM((length, BLOCK), F32),
            pltpu.VMEM((heads, length), F32),
            pltpu.VMEM((heads, length), F32),
            pltpu.VMEM((2 * blocks + 2, 8, width), F32),
            pltpu.VMEM((STATE, CHUNK), F32),
            pltpu.VMEM((STATE, width), BF16),
            pltpu.VMEM((length, width), F32),
            pltpu.VMEM((length, width), F32),
            pltpu.VMEM((length, width), BF16),
            pltpu.VMEM((STATE, width), BF16),
            pltpu.VMEM((8, width), F32),
            pltpu.VMEM((width, STATE), BF16),
            pltpu.VMEM((chunks // 2, SPAN * ROW, 4, piece, STATE), BF16),
            pltpu.VMEM((SPAN * ROW * 4, piece, STATE), BF16),
            pltpu.VMEM((chunks // 2, plane, piece, STATE), BF16),
            pltpu.VMEM((chunks, plane // ROW, ROW, piece, STATE), BF16),
            pltpu.VMEM((plane // ROW, ROW, piece, STATE), BF16),
            pltpu.SMEM((plane,), jnp.int32),
            pltpu.VMEM((heads, length), F32),
            pltpu.VMEM((STATE, width), BF16),
            pltpu.VMEM((ranks - 1, length // ranks, CHUNK), BF16),
            pltpu.VMEM((ranks - 1, length // ranks, STATE), BF16),
            pltpu.VMEM((ranks - 1, 8, length // ranks), F32),
            pltpu.VMEM((ranks - 1, STATE, CHUNK), BF16),
            dma((4,)),
            dma((chunks,)),
            dma((chunks,)),
            dma((chunks // 2,)),
            dma((chunks // 2,)),
            dma((chunks,)),
            dma((2,)),
            dma((chunks,)),
            dma((chunks,)),
            dma((chunks,)),
            dma((chunks,)),
            dma((chunks, ranks - 1)),
            dma((chunks, ranks - 1)),
            dma((chunks,)),
            dma((ranks - 1, 2)),
            dma((ranks - 1, 2)),
            dma((ranks - 1,)),
            dma((ranks - 1,)),
            dma((ranks - 1,)),
            dma((ranks - 1,)),
            dma((ranks - 1,)),
        ],
        compiler_params=pltpu.CompilerParams(
            collective_id=0, has_side_effects=True, vmem_limit_bytes=56 * 2**20
        ),
        name="scan_and_send",
    )(
        first_snap,
        prefix_kilo,
        snap_slot,
        tokens[0],
        input_map[0],
        output_map[0],
        log_decay[0],
        step_size[0],
        skip_gain.reshape(1, heads),
        snapshots.reshape(snapshots.shape[0], width, STATE),
    )
    parts = 4
    result = pl.pallas_call(
        functools.partial(copy_kernel, parts),
        out_shape=jax.ShapeDtypeStruct(out_shape, BF16),
        in_specs=[pl.BlockSpec(memory_space=pl.ANY)],
        out_specs=pl.BlockSpec(memory_space=pl.ANY),
        scratch_shapes=[
            pltpu.VMEM(out_shape, BF16),
            pltpu.SemaphoreType.DMA((parts,)),
            pltpu.SemaphoreType.DMA((parts,)),
        ],
        compiler_params=pltpu.CompilerParams(vmem_limit_bytes=60 * 2**20),
        name="place_result",
    )(mixed)
    return result[None]


def solution(mesh):
    placed = (
        P("dp", "seq", "tensor"),
        P("dp", "seq", "tensor"),
        P("dp", "seq", "tensor"),
        P("dp", "tensor", "seq"),
        P("dp", "tensor", "seq"),
        P("tensor"),
        P(("dp", "seq"), "tensor", None, None),
        P(),
        P(),
        P(),
    )
    return jax.shard_map(
        per_device,
        mesh=mesh,
        in_specs=placed,
        out_specs=P("dp", ("seq", "tensor"), None),
        check_vma=False,
    )
```
